256 devices in a mesh: fx: 16 (over z_hi, x), fy: 16 (over z_lo, y, core).
Axes of the slice: x: 4, y: 4, z: 8 (z_hi: 4, z_lo: 2; z = z_hi * 2 + z_lo), core: 2. Of those that a mesh axis runs over, the one named last changes fastest.
Arguments:
- features: bfloat16 [12, 256, 256, 128], P(None, 'fx', 'fy'), may hold values from -6 to 6
- weight: bfloat16 [3, 3, 128, 128], replicated, may hold values from -0.1875 to 0.1875
- out_bias: float32 [128], replicated, may hold values from -3 to 3
- cotangent: bfloat16 [12, 256, 256, 128], P(None, 'fx', 'fy'), may hold values from -6 to 6
- seam_face: int32 [12, 4], replicated, may hold values from 0 to 11, as said below
- seam_edge: int32 [12, 4], replicated, may hold values from 0 to 3, as said below
- seam_flip: int32 [12, 4], replicated, may hold values from 0 to 1, as said below
Outputs:
- activated: bfloat16 [12, 256, 256, 128], P(None, 'fx', 'fy')
- gradient: bfloat16 [12, 256, 256, 128], P(None, 'fx', 'fy')
The draws below stay inside these ranges and needn't reach their ends.
Inputs may be any that keep to these rules, and one draw needn't show every extreme that they name: seam_face and seam_edge pair all 48 edges two by two in an arbitrary pairing (two edges of one face may be glued): the edge glued to edge (seam_face[f, e], seam_edge[f, e]) is (f, e) again, and no edge is glued to itself. `seam_edge`: edge codes: 0 row 0, 1 last row, 2 column 0, 3 last column. `seam_flip`: both edges of a glued pair carry the same value.
All inputs are finite; a program needn't handle non-finite values.
Results may differ from the reference program's by a relative error of at most 0.0049.
Values may be sent and summed in bfloat16 or wider, within the bound.
A program may use at most 64 MiB of HBM per device.

```python
import jax
import jax.numpy as jnp
from jax import lax

C = 128
FACES = 12
NSIDE = 256


def seam_tables(key):
    inner_key = jax.random.fold_in(key, 7)
    edge_order = jax.random.permutation(inner_key, FACES * 4).astype(jnp.int32)
    first_half = edge_order[0::2]
    second_half = edge_order[1::2]
    partner = jnp.zeros((FACES * 4,), jnp.int32).at[first_half].set(second_half).at[second_half].set(first_half)
    turn_bits = jax.random.randint(jax.random.fold_in(inner_key, 3), (FACES * 2,), 0, 2).astype(jnp.int32)
    turn_bits = turn_bits.at[0].set(1).at[1].set(0)
    flip_bits = jnp.zeros((FACES * 4,), jnp.int32).at[first_half].set(turn_bits).at[second_half].set(turn_bits)
    return (partner, flip_bits)


def draw_seam_face(key, part):
    partner, flip_bits = seam_tables(key)
    return (partner // 4).reshape(FACES, 4)


def draw_seam_edge(key, part):
    partner, flip_bits = seam_tables(key)
    return (partner % 4).reshape(FACES, 4)


def draw_seam_flip(key, part):
    partner, flip_bits = seam_tables(key)
    return flip_bits.reshape(FACES, 4)


def level_of(rng, dims, shards, low, largest):
    gain = 1.0
    for position, parts in shards:
        draws = jax.random.uniform(jax.random.fold_in(jax.random.fold_in(rng, 6), position), (parts,), jnp.float32, low / len(shards), largest / len(shards))
        gain = gain * jnp.repeat(jnp.exp(draws), dims[position] // parts).reshape((-1,) + (1,) * (len(dims) - 1 - position))
    return gain


def bell_draw(own_key, extent, width, limit, split=(), kind=jnp.bfloat16):
    drawn = jax.random.normal(own_key, extent, jnp.float32) * width
    if len(split) > 0:
        drawn = level_of(own_key, extent, split, -0.22, 0.18) * drawn
    return jnp.clip(drawn, min=-limit, max=limit).astype(kind)


def setup_inputs(seed: int = 0) -> dict:
    key_of = jax.random.split(jax.random.key(seed), 8)
    return {
        "features": bell_draw(key_of[0], (FACES, NSIDE, NSIDE, C), 1.0, 6.0, ((1, 16), (2, 16))),
        "weight": bell_draw(key_of[1], (3, 3, C, C), (9 * C) ** -0.5, 0.1875),
        "out_bias": bell_draw(key_of[2], (C,), 0.5, 3.0, (), jnp.float32),
        "cotangent": bell_draw(key_of[3], (FACES, NSIDE, NSIDE, C), 1.0, 6.0, ((1, 16), (2, 16))),
        "seam_face": draw_seam_face(jax.random.fold_in(key_of[7], 71), 0),
        "seam_edge": draw_seam_edge(jax.random.fold_in(key_of[7], 71), 0),
        "seam_flip": draw_seam_flip(jax.random.fold_in(key_of[7], 71), 0),
    }


def silu_slope(value):
    sigma = jax.nn.sigmoid(value)
    return sigma * (1.0 + value * (1.0 - sigma))


def tap_window(source, weight, row_start, col_start, row_total, col_total, adjoint):
    channels = source.shape[-1]
    summed = jnp.zeros((row_total * col_total, channels), jnp.float32)
    for tap_row in range(3):
        for tap_col in range(3):
            if adjoint:
                row_from = row_start + 2 - tap_row
                col_from = col_start + 2 - tap_col
                matrix = jnp.transpose(weight[tap_row, tap_col])
            else:
                row_from = row_start + tap_row
                col_from = col_start + tap_col
                matrix = weight[tap_row, tap_col]
            window = source[row_from:row_from + row_total, col_from:col_from + col_total]
            window = window.reshape(row_total * col_total, channels)
            summed = summed + jnp.dot(window, matrix, preferred_element_type=jnp.float32)
    return summed.reshape(row_total, col_total, channels)


def border_lines(features):
    return jnp.stack([features[:, 0], features[:, -1], features[:, :, 0], features[:, :, -1]], axis=1)


def oriented(edge_lines, seam_face, seam_edge, seam_flip, positions):
    side_len = edge_lines.shape[2]
    turned = jnp.where(seam_flip[:, :, None] == 1, side_len - 1 - positions[None, None, :], positions[None, None, :])
    return edge_lines[seam_face[:, :, None], seam_edge[:, :, None], turned]


def corner_values(edge_lines, seam_face, seam_edge, seam_flip):
    side_len = edge_lines.shape[2]
    end_values = oriented(edge_lines, seam_face, seam_edge, seam_flip, jnp.array([0, side_len - 1], jnp.int32))
    end_values = end_values.astype(jnp.float32)
    north_west = (0.5 * (end_values[:, 0, 0] + end_values[:, 2, 0])).astype(jnp.bfloat16)
    north_east = (0.5 * (end_values[:, 0, 1] + end_values[:, 3, 0])).astype(jnp.bfloat16)
    south_west = (0.5 * (end_values[:, 1, 0] + end_values[:, 2, 1])).astype(jnp.bfloat16)
    south_east = (0.5 * (end_values[:, 1, 1] + end_values[:, 3, 1])).astype(jnp.bfloat16)
    return north_west, north_east, south_west, south_east


def split_corners(cycle_line):
    inner = cycle_line[1:-1]
    inner = inner.at[0].add(0.5 * cycle_line[0])
    inner = inner.at[-1].add(0.5 * cycle_line[-1])
    return inner


def reference(features, weight, out_bias, cotangent, seam_face, seam_edge, seam_flip):
    side_len = features.shape[1]
    edge_lines = border_lines(features)
    positions = jnp.arange(side_len, dtype=jnp.int32)
    seam_values = oriented(edge_lines, seam_face, seam_edge, seam_flip, positions)
    north_west, north_east, south_west, south_east = corner_values(edge_lines, seam_face, seam_edge, seam_flip)

    def forward_face(inputs):
        face_data, face_seams, corner_nw, corner_ne, corner_sw, corner_se, cot_face = inputs
        top_row = jnp.concatenate([corner_nw[None], face_seams[0], corner_ne[None]], 0)
        bottom_row = jnp.concatenate([corner_sw[None], face_seams[1], corner_se[None]], 0)
        middle = jnp.concatenate([face_seams[2][:, None], face_data, face_seams[3][:, None]], 1)
        padded = jnp.concatenate([top_row[None], middle, bottom_row[None]], 0)
        preact = tap_window(padded, weight, 0, 0, side_len, side_len, False) + out_bias
        activated = jax.nn.silu(preact).astype(jnp.bfloat16)
        slope = (cot_face.astype(jnp.float32) * silu_slope(preact)).astype(jnp.bfloat16)
        grad_padded = jnp.pad(slope, ((2, 2), (2, 2), (0, 0)))
        cycle_top = tap_window(grad_padded, weight, 0, 0, 1, side_len + 2, True)[0]
        cycle_bottom = tap_window(grad_padded, weight, side_len + 1, 0, 1, side_len + 2, True)[0]
        cycle_left = tap_window(grad_padded, weight, 0, 0, side_len + 2, 1, True)[:, 0]
        cycle_right = tap_window(grad_padded, weight, 0, side_len + 1, side_len + 2, 1, True)[:, 0]
        cycle_parts = jnp.stack([split_corners(cycle_top), split_corners(cycle_bottom),
                                split_corners(cycle_left), split_corners(cycle_right)], 0)
        return activated, slope, cycle_parts.astype(jnp.bfloat16)

    activated, slope, cycle_parts = lax.map(
        forward_face, (features, seam_values, north_west, north_east, south_west, south_east, cotangent))
    returns = oriented(cycle_parts, seam_face, seam_edge, seam_flip, positions).astype(jnp.float32)

    def adjoint_face(inputs):
        slope_face, back_lines = inputs
        grad_padded = jnp.pad(slope_face, ((2, 2), (2, 2), (0, 0)))
        inner = tap_window(grad_padded, weight, 1, 1, side_len, side_len, True)
        inner = inner.at[0].add(back_lines[0])
        inner = inner.at[-1].add(back_lines[1])
        inner = inner.at[:, 0].add(back_lines[2])
        inner = inner.at[:, -1].add(back_lines[3])
        return inner.astype(jnp.bfloat16)

    gradient = lax.map(adjoint_face, (slope, returns))
    return activated, gradient
```

```python
import functools

import jax
import jax.numpy as jnp
from jax import lax
from jax.experimental import pallas as pl
from jax.experimental.pallas import tpu as pltpu
from jax.sharding import PartitionSpec as P

MESH = pl.DeviceIdType.MESH
F32 = jnp.float32
BF16 = jnp.bfloat16


def dot(a, b):
    return jnp.dot(a, b, preferred_element_type=F32)


def rows_iota(shape):
    return lax.broadcasted_iota(jnp.int32, shape, 0)


def cols_iota(shape):
    return lax.broadcasted_iota(jnp.int32, shape, 1)


def shifted_sum(taps, run):
    total, width = taps.shape[0], taps.shape[1] // 3
    place = rows_iota((total, width)) % run
    below = jnp.where(place == 0, 0.0, pltpu.roll(taps[:, :width], 1, 0))
    above = jnp.where(place == run - 1, 0.0, pltpu.roll(taps[:, 2 * width:], total - 1, 0))
    return taps[:, width:2 * width] + below + above


def silu_parts(value):
    sigma = 1.0 / (1.0 + jnp.exp(-value))
    return value * sigma, sigma * (1.0 + value * (1.0 - sigma))


def kernel(nx, ny, faces, side, width,
           face_tab, edge_tab, flip_tab, bias_ref, x_hbm, w_hbm, cot_hbm,
           act_out, grad_out,
           xp, cot, w9, acc, sp, act, grad,
           wf, wcol, vf, vcol, colcot, ring,
           src, corner_src, strip_in, corner_in, seam_a, seam_b, seam_c, seam_d, ends,
           near_send, near_recv, seam_send, seam_recv, ends_send, ends_recv, load_sem, store_sem):
    x = lax.axis_index("fx")
    y = lax.axis_index("fy")
    top, bottom, left, right = x == 0, x == nx - 1, y == 0, y == ny - 1
    row_rim = jnp.logical_or(top, bottom)
    col_rim = jnp.logical_or(left, right)
    seam = ((seam_a, seam_b), (seam_c, seam_d))
    cells = side * side
    strip = faces * side
    row_edge = x // (nx - 1)
    col_edge = 2 + y // (ny - 1)
    rims = ((row_rim, row_edge, y, ny), (col_rim, col_edge, x, nx))

    near = []
    for dx, dy, slot in ((-1, 0, 0), (1, 0, 1), (0, -1, 2), (0, 1, 3), (-1, -1, 4), (-1, 1, 5), (1, -1, 6), (1, 1, 7)):
        tx, ty = x + dx, y + dy
        inside = None
        for ok in ([tx >= 0] if dx < 0 else [tx < nx] if dx > 0 else []) + ([ty >= 0] if dy < 0 else [ty < ny] if dy > 0 else []):
            inside = ok if inside is None else jnp.logical_and(inside, ok)
        back = slot ^ 1 if slot < 4 else 4 + (3 - (slot - 4))
        near.append((tx, ty, inside, slot, back))

    def seam_target(kind, count, place, step):
        half, turn = step // 2, step % 2
        spot = place + turn * (count - 1 - 2 * place)
        if kind == 0:
            tx, ty = half * (nx - 1), spot
        else:
            tx, ty = spot, half * (ny - 1)
        mine = jnp.logical_and(tx == x, ty == y)
        return turn, tx, ty, mine

    def ends_target(kind, count, place, step):
        half, end, turn = step // 4, (step // 2) % 2, step % 2
        cell = (end + turn + 1) % 2
        spot = place + 1 - 2 * end + turn * (count - 1 - 2 * place)
        valid = jnp.logical_and(spot >= 0, spot < count)
        if kind == 0:
            tx, ty = half * (nx - 1), spot
        else:
            tx, ty = spot, half * (ny - 1)
        mine = jnp.logical_and(tx == x, ty == y)
        return end, turn, cell, tx, ty, valid, mine

    def near_copy(trip, item):
        tx, ty, inside, slot, back = item
        if slot < 4:
            source, target = src.at[trip, 0, slot], strip_in.at[trip, back]
        else:
            source, target = corner_src.at[trip, slot - 4], corner_in.at[trip, back - 4]
        return pltpu.make_async_remote_copy(
            src_ref=source, dst_ref=target, send_sem=near_send.at[trip, slot], recv_sem=near_recv.at[trip, back],
            device_id=(tx, ty), device_id_type=MESH)

    def near_arrival(trip, slot):
        here = strip_in.at[trip, slot] if slot < 4 else corner_in.at[trip, slot - 4]
        return pltpu.make_async_copy(here, here, near_recv.at[trip, slot])

    def seam_copy(away, trip, rim, edge, kind, step, turn, tx, ty):
        source = src.at[trip, turn, edge]
        target = seam[trip][kind].at[turn, edge]
        if not away:
            return pltpu.make_async_copy(source, target, seam_recv.at[trip, kind])
        return pltpu.make_async_remote_copy(
            src_ref=source, dst_ref=target, send_sem=seam_send.at[trip, rim, kind, step],
            recv_sem=seam_recv.at[trip, kind], device_id=(tx, ty), device_id_type=MESH)

    def ends_copy(away, trip, rim, edge, kind, step, end, turn, cell, tx, ty):
        which = 2 * edge + cell if rim == 0 else edge - 2 + 2 * cell
        source = corner_src.at[trip, which]
        target = ends.at[trip, kind, end, turn, edge]
        if not away:
            return pltpu.make_async_copy(source, target, ends_recv.at[trip, kind, end])
        return pltpu.make_async_remote_copy(
            src_ref=source, dst_ref=target, send_sem=ends_send.at[trip, rim, kind, step],
            recv_sem=ends_recv.at[trip, kind, end], device_id=(tx, ty), device_id_type=MESH)

    def each_far(act_on):
        for rim, (active, edge, place, count) in enumerate(rims):
            @pl.when(active)
            def _(rim=rim, edge=edge, place=place, count=count):
                for kind in range(2):
                    def seam_step(step, carry, kind=kind):
                        turn, tx, ty, mine = seam_target(kind, count, place, step)
                        act_on("seam", rim, edge, kind, step, (turn, tx, ty), None, mine)
                        return carry
                    lax.fori_loop(0, 4, seam_step, 0)
                for kind in range(2):
                    def ends_step(step, carry, kind=kind):
                        end, turn, cell, tx, ty, valid, mine = ends_target(kind, count, place, step)
                        act_on("ends", rim, edge, kind, step, (end, turn, cell, tx, ty), valid, mine)
                        return carry
                    lax.fori_loop(0, 8, ends_step, 0)

    def send_all(trip):
        for item in near:
            @pl.when(item[2])
            def _(item=item):
                near_copy(trip, item).start()

        def begin(sort, rim, edge, kind, step, rest, valid, mine):
            copy = seam_copy if sort == "seam" else ends_copy
            far_on = jnp.logical_not(mine)
            if valid is not None:
                far_on = jnp.logical_and(far_on, valid)
                mine = jnp.logical_and(mine, valid)

            @pl.when(far_on)
            def _():
                copy(True, trip, rim, edge, kind, step, *rest).start()

            @pl.when(mine)
            def _():
                copy(False, trip, rim, edge, kind, step, *rest).start()

        each_far(begin)

    def wait_sent(trip):
        for item in near:
            @pl.when(item[2])
            def _(item=item):
                near_copy(trip, item).wait_send()

        def finish(sort, rim, edge, kind, step, rest, valid, mine):
            copy = seam_copy if sort == "seam" else ends_copy
            far_on = jnp.logical_not(mine)
            if valid is not None:
                far_on = jnp.logical_and(far_on, valid)

            @pl.when(far_on)
            def _():
                copy(True, trip, rim, edge, kind, step, *rest).wait_send()

        each_far(finish)

    first_last = jnp.where(
        jnp.logical_and(
            cols_iota((32, strip)) == (rows_iota((32, strip)) % 16) * side + (rows_iota((32, strip)) // 16) * (side - 1),
            rows_iota((32, strip)) % 16 < faces),
        1.0, 0.0).astype(BF16)

    def turned(trip):
        def turn_one(edge):
            back = rows_iota((strip, strip)) - 2 * (rows_iota((strip, strip)) % side) + (side - 1)
            turner = jnp.where(back == cols_iota((strip, strip)), 1.0, 0.0).astype(BF16)
            line = src[trip, 0, edge].reshape(strip, width)
            src[trip, 1, edge] = dot(turner, line).astype(BF16).reshape(faces, side, width)

        @pl.when(row_rim)
        def _():
            turn_one(row_edge)

        @pl.when(col_rim)
        def _():
            turn_one(col_edge)

    def arrivals(trip):
        for item in near:
            @pl.when(item[2])
            def _(item=item):
                near_arrival(trip, item[3]).wait()
        for rim, (active, edge, place, count) in enumerate(rims):
            @pl.when(active)
            def _(rim=rim, edge=edge, place=place, count=count):
                whole = seam[trip][rim]
                pltpu.make_async_copy(whole, whole, seam_recv.at[trip, rim]).wait()

                def pick(f, carry):
                    strip_in[trip, edge, f] = seam[trip][rim][flip_tab[f, edge], edge_tab[f, edge], face_tab[f, edge]]
                    return carry
                lax.fori_loop(0, faces, pick, 0)

                chosen = jnp.zeros((16, 128), F32)
                for f in range(faces):
                    code = (flip_tab[f, edge] * 4 + edge_tab[f, edge]) * 16 + face_tab[f, edge]
                    hit = jnp.logical_and(rows_iota((16, 128)) == f, cols_iota((16, 128)) == code)
                    chosen = jnp.where(hit, 1.0, chosen)
                chosen = chosen.astype(BF16)
                for end in range(2):
                    @pl.when(place > 0 if end == 0 else place < count - 1)
                    def _(end=end):
                        part = ends.at[trip, rim, end]
                        pltpu.make_async_copy(part, part, ends_recv.at[trip, rim, end]).wait()
                        value = dot(chosen, ends[trip, rim, end].reshape(128, width)).astype(BF16)
                        if rim == 0:
                            corner_in[trip, 2 * edge + end] = value
                        else:
                            corner_in[trip, edge - 2 + 2 * end] = value

        @pl.when(jnp.logical_and(row_rim, col_rim))
        def _():
            which = 2 * row_edge + col_edge - 2
            if trip == 0:
                ends_a = dot(first_last, strip_in[0, row_edge].reshape(strip, width))
                ends_b = dot(first_last, strip_in[0, col_edge].reshape(strip, width))
                at_a = jnp.where(left, ends_a[:16], ends_a[16:])
                at_b = jnp.where(top, ends_b[:16], ends_b[16:])
                corner_in[0, which] = (0.5 * (at_a + at_b)).astype(BF16)
            else:
                corner_in[1, which] = jnp.zeros((16, width), BF16)

    load_x = pltpu.make_async_copy(x_hbm, xp.at[:, 1:side + 1], load_sem.at[0])
    load_w = pltpu.make_async_copy(w_hbm, w9, load_sem.at[1])
    load_c = pltpu.make_async_copy(cot_hbm, cot, load_sem.at[2])
    load_x.start()
    load_w.start()
    load_c.start()

    barrier = pltpu.get_barrier_semaphore()
    due = jnp.int32(0)
    for tx, ty, inside, slot, back in near:
        @pl.when(inside)
        def _(tx=tx, ty=ty):
            pl.semaphore_signal(barrier, inc=1, device_id=(tx, ty), device_id_type=MESH)
        due = due + inside.astype(jnp.int32)
    for rim, (active, edge, place, count) in enumerate(rims):
        def signal_if(on, tx, ty):
            @pl.when(on)
            def _():
                pl.semaphore_signal(barrier, inc=1, device_id=(tx, ty), device_id_type=MESH)
        for kind in range(2):
            def seam_step(step, total, kind=kind, active=active, place=place, count=count):
                turn, tx, ty, mine = seam_target(kind, count, place, step)
                on = jnp.logical_and(active, jnp.logical_not(mine))
                signal_if(on, tx, ty)
                return total + on.astype(jnp.int32)
            due = lax.fori_loop(0, 4, seam_step, due)

            def ends_step(step, total, kind=kind, active=active, place=place, count=count):
                end, turn, cell, tx, ty, valid, mine = ends_target(kind, count, place, step)
                on = jnp.logical_and(jnp.logical_and(active, valid), jnp.logical_not(mine))
                signal_if(on, tx, ty)
                return total + on.astype(jnp.int32)
            due = lax.fori_loop(0, 8, ends_step, due)

    zero_rows = jnp.zeros((faces, side, width), BF16)
    xp[:, 0] = zero_rows
    xp[:, side + 1] = zero_rows
    sp[:, 0] = zero_rows
    sp[:, side + 1] = zero_rows
    load_x.wait()
    src[0, 0, 0] = xp[:, 1]
    src[0, 0, 1] = xp[:, side]
    column_pick = jnp.where(
        cols_iota((2 * side, cells)) == (rows_iota((2 * side, cells)) % side) * side
        + (rows_iota((2 * side, cells)) // side) * (side - 1), 1.0, 0.0).astype(BF16)
    for f in range(faces):
        both = dot(column_pick, xp[f, 1:side + 1].reshape(cells, width)).astype(BF16)
        src[0, 0, 2, f] = both[:side]
        src[0, 0, 3, f] = both[side:]
    for half in range(2):
        picked = dot(first_last, src[0, 0, half].reshape(strip, width)).astype(BF16)
        corner_src[0, 2 * half] = picked[:16]
        corner_src[0, 2 * half + 1] = picked[16:]
    turned(0)
    pl.semaphore_wait(barrier, due)
    send_all(0)

    load_w.wait()
    for a in range(3):
        for b in range(3):
            tap = w9[a, b]
            back = tap.astype(F32).T.astype(BF16)
            wf[a * width:(a + 1) * width, b * width:(b + 1) * width] = tap
            vf[(2 - a) * width:(3 - a) * width, (2 - b) * width:(3 - b) * width] = back
            if b != 1:
                wcol[b // 2, :, a * width:(a + 1) * width] = tap
                vcol[b // 2, :, (2 - a) * width:(3 - a) * width] = back
    load_c.wait()
    for f in range(faces):
        both = dot(column_pick, cot[f].reshape(cells, width))
        colcot[0, f * side:(f + 1) * side] = both[:side]
        colcot[1, f * side:(f + 1) * side] = both[side:]

    def conv(source, f, weights):
        stacked = jnp.concatenate(
            [source[f, a:a + side].reshape(cells, width) for a in range(3)], axis=1)
        return shifted_sum(dot(stacked, weights), side)

    def forward_face(f, carry):
        acc[pl.ds(pl.multiple_of(f * cells, cells), cells)] = conv(xp, f, wf[...]) + bias_ref[...]
        return carry
    lax.fori_loop(0, faces, forward_face, 0)

    def add_rim(strips, corners):
        for half in range(2):
            line = strips[half]
            for f in range(faces):
                at = f * cells + half * (cells - side)
                acc[at:at + side] += line[f * side:(f + 1) * side]
        for half in range(2):
            at = pl.ds(half * (side - 1), strip, stride=side)
            acc[at] = acc[at] + strips[2 + half]
        for which in range(4):
            at = pl.ds((which // 2) * (cells - side) + (which % 2) * (side - 1), faces, stride=cells)
            acc[at] = acc[at] + corners[which]

    arrivals(0)
    strips = []
    for edge in range(4):
        line = strip_in[0, edge].reshape(strip, width)
        weights = wf[2 * edge * width:(2 * edge + 1) * width] if edge < 2 else wcol[edge - 2]
        strips.append(shifted_sum(dot(line, weights), side))
    corners = [dot(corner_in[0, 2 * a + b], w9[2 * a, 2 * b])[:faces] for a in range(2) for b in range(2)]
    add_rim(strips, corners)

    rim_slopes = []
    for half in range(2):
        at = half * (cells - side)
        line = jnp.concatenate([acc[f * cells + at:f * cells + at + side] for f in range(faces)], axis=0)
        rim_slopes.append((cot[:, half * (side - 1)].reshape(strip, width).astype(F32) * silu_parts(line)[1]).astype(BF16))
    for half in range(2):
        line = acc[pl.ds(half * (side - 1), strip, stride=side)]
        rim_slopes.append((colcot[half] * silu_parts(line)[1]).astype(BF16))
    for edge in range(4):
        weights = vf[2 * (1 - edge) * width:(2 * (1 - edge) + 1) * width] if edge < 2 else vcol[edge - 2]
        ring[edge] = shifted_sum(dot(rim_slopes[edge], weights), side)
    for a in range(2):
        picked = dot(first_last, rim_slopes[a]).astype(BF16)
        for b in range(2):
            beyond = dot(picked[16 * b:16 * b + 16], vf[2 * (1 - a) * width:(2 * (1 - a) + 1) * width,
                                                        2 * (1 - b) * width:(2 * (1 - b) + 1) * width])
            corner_src[1, 2 * a + b] = beyond.astype(BF16)

            @pl.when(jnp.logical_and(bottom if a else top, right if b else left))
            def _(a=a, b=b, beyond=beyond):
                along_row = pl.ds(b * (side - 1), faces, stride=side)
                along_col = pl.ds(a * (side - 1), faces, stride=side)
                ring[a, along_row] = ring[a, along_row] + 0.5 * beyond[:faces]
                ring[2 + b, along_col] = ring[2 + b, along_col] + 0.5 * beyond[:faces]
    for edge in range(4):
        src[1, 0, edge] = ring[edge].astype(BF16).reshape(faces, side, width)
    turned(1)
    send_all(1)

    def adjoint_face(f, carry):
        at = pl.ds(pl.multiple_of(f * cells, cells), cells)
        value, slope = silu_parts(acc[at])
        act[f] = value.astype(BF16).reshape(side, side, width)
        slope = cot[f].reshape(cells, width).astype(F32) * slope
        sp[f, 1:side + 1] = slope.astype(BF16).reshape(side, side, width)
        acc[at] = conv(sp, f, vf[...])
        return carry
    lax.fori_loop(0, faces, adjoint_face, 0)
    store_act = pltpu.make_async_copy(act, act_out, store_sem.at[0])
    store_act.start()

    arrivals(1)
    add_rim([strip_in[1, edge].reshape(strip, width).astype(F32) for edge in range(4)],
            [corner_in[1, which].astype(F32)[:faces] for which in range(4)])

    def finish_face(f, carry):
        at = pl.ds(pl.multiple_of(f * cells, cells), cells)
        grad[f] = acc[at].astype(BF16).reshape(side, side, width)
        return carry
    lax.fori_loop(0, faces, finish_face, 0)
    store_grad = pltpu.make_async_copy(grad, grad_out, store_sem.at[1])
    store_grad.start()
    wait_sent(0)
    wait_sent(1)
    store_act.wait()
    store_grad.wait()


def shards(features, weight, out_bias, cotangent, seam_face, seam_edge, seam_flip):
    faces, side, _, width = features.shape
    nx, ny = lax.axis_size("fx"), lax.axis_size("fy")
    patch = (faces, side, side, width)
    padded = (faces, side + 2, side, width)
    strip = faces * side
    dma = pltpu.SemaphoreType.DMA
    anywhere = pl.BlockSpec(memory_space=pl.ANY)
    table = pl.BlockSpec(memory_space=pltpu.SMEM)
    return pl.pallas_call(
        functools.partial(kernel, nx, ny, faces, side, width),
        out_shape=(jax.ShapeDtypeStruct(patch, BF16), jax.ShapeDtypeStruct(patch, BF16)),
        in_specs=[table, table, table, pl.BlockSpec(memory_space=pltpu.VMEM), anywhere, anywhere, anywhere],
        out_specs=(anywhere, anywhere),
        scratch_shapes=[
            pltpu.VMEM(padded, BF16),
            pltpu.VMEM(patch, BF16),
            pltpu.VMEM((3, 3, width, width), BF16),
            pltpu.VMEM((faces * side * side, width), F32),
            pltpu.VMEM(padded, BF16),
            pltpu.VMEM(patch, BF16),
            pltpu.VMEM(patch, BF16),
            pltpu.VMEM((3 * width, 3 * width), BF16),
            pltpu.VMEM((2, width, 3 * width), BF16),
            pltpu.VMEM((3 * width, 3 * width), BF16),
            pltpu.VMEM((2, width, 3 * width), BF16),
            pltpu.VMEM((2, strip, width), F32),
            pltpu.VMEM((4, strip, width), F32),
            pltpu.VMEM((2, 2, 4, faces, side, width), BF16),
            pltpu.VMEM((2, 4, 16, width), BF16),
            pltpu.VMEM((2, 4, faces, side, width), BF16),
            pltpu.VMEM((2, 4, 16, width), BF16),
            *[pltpu.VMEM((2, 4, faces, side, width), BF16)] * 4,
            pltpu.VMEM((2, 2, 2, 2, 4, 16, width), BF16),
            dma((2, 8)),
            dma((2, 8)),
            dma((2, 2, 2, 4)),
            dma((2, 2)),
            dma((2, 2, 2, 8)),
            dma((2, 2, 2)),
            dma((3,)),
            dma((2,)),
        ],
        compiler_params=pltpu.CompilerParams(
            collective_id=0, has_side_effects=True, vmem_limit_bytes=40 * 1024 * 1024),
    )(seam_face, seam_edge, seam_flip, out_bias.reshape(1, width), features, weight, cotangent)


def solution(mesh):
    in_specs = (P(None, "fx", "fy", None), P(), P(), P(None, "fx", "fy", None), P(), P(), P())
    out_specs = (P(None, "fx", "fy", None), P(None, "fx", "fy", None))
    return jax.shard_map(shards, mesh=mesh, in_specs=in_specs, out_specs=out_specs, check_vma=False)
```

```python
import functools

import jax
import jax.numpy as jnp
from jax import lax
from jax.experimental import pallas as pl
from jax.experimental.pallas import tpu as pltpu
from jax.sharding import PartitionSpec as P

MESH = pl.DeviceIdType.MESH
F32 = jnp.float32
BF16 = jnp.bfloat16


def dot(a, b):
    return jnp.dot(a, b, preferred_element_type=F32)


def rows_iota(shape):
    return lax.broadcasted_iota(jnp.int32, shape, 0)


def cols_iota(shape):
    return lax.broadcasted_iota(jnp.int32, shape, 1)


def shifted_sum(taps, run):
    total, width = taps.shape[0], taps.shape[1] // 3
    place = rows_iota((total, width)) % run
    below = jnp.where(place == 0, 0.0, pltpu.roll(taps[:, :width], 1, 0))
    above = jnp.where(place == run - 1, 0.0, pltpu.roll(taps[:, 2 * width:], total - 1, 0))
    return taps[:, width:2 * width] + below + above


def silu_parts(value):
    sigma = 1.0 / (1.0 + jnp.exp(-value))
    return value * sigma, sigma * (1.0 + value * (1.0 - sigma))


def kernel(nx, ny, faces, side, width,
           face_hbm, edge_hbm, flip_hbm, bias_hbm, x_hbm, w_hbm, cot_hbm,
           act, grad,
           face_tab, edge_tab, flip_tab, bias_ref, xp, cot, w9, acc, sp,
           wf, wcol, vf, vcol, colcot, ring, turner, chooser,
           src, corner_src, strip_in, corner_in, seam_first, seam_second, end_src,
           near_send, near_recv, seam_send, seam_recv, ends_send, load_sem):
    x = lax.axis_index("fx")
    y = lax.axis_index("fy")
    top, bottom, left, right = x == 0, x == nx - 1, y == 0, y == ny - 1
    row_rim = jnp.logical_or(top, bottom)
    col_rim = jnp.logical_or(left, right)
    rim = jnp.logical_or(row_rim, col_rim)
    corner = jnp.logical_and(row_rim, col_rim)
    seam = (seam_first, seam_second)
    cells = side * side
    strip = faces * side
    row_edge = x // (nx - 1)
    col_edge = 2 + y // (ny - 1)
    rims = ((row_rim, row_edge, y, ny, (y // (ny // 2)) * 4 + row_edge),
            (col_rim, col_edge, x, nx, (x // (nx // 2)) * 4 + col_edge))

    near = []
    for dx, dy, slot in ((-1, 0, 0), (1, 0, 1), (0, -1, 2), (0, 1, 3), (-1, -1, 4), (-1, 1, 5), (1, -1, 6), (1, 1, 7)):
        tx, ty = x + dx, y + dy
        inside = None
        for ok in ([tx >= 0] if dx < 0 else [tx < nx] if dx > 0 else []) + ([ty >= 0] if dy < 0 else [ty < ny] if dy > 0 else []):
            inside = ok if inside is None else jnp.logical_and(inside, ok)
        back = slot ^ 1 if slot < 4 else 4 + (3 - (slot - 4))
        near.append((tx, ty, inside, slot, back))

    def partners(which):
        active, edge, place, count, slot = rims[which]
        for kind in range(2):
            for half in range(2):
                for turn in range(2):
                    spot = count - 1 - place if turn else place
                    tx, ty = (half * (nx - 1), spot) if kind == 0 else (spot, half * (ny - 1))
                    other = jnp.logical_not(jnp.logical_and(tx == x, ty == y))
                    on = jnp.logical_and(active, other)
                    if kind == 1:
                        on = jnp.logical_and(on, jnp.logical_not(corner))
                    yield kind * 4 + half * 2 + turn, tx, ty, on

    def near_copy(trip, item):
        tx, ty, inside, slot, back = item
        if slot < 4:
            source, target = src.at[trip, slot], strip_in.at[trip, back]
        else:
            source, target = corner_src.at[trip, slot - 4], corner_in.at[trip, back - 4]
        return pltpu.make_async_remote_copy(
            src_ref=source, dst_ref=target, send_sem=near_send.at[trip, slot], recv_sem=near_recv.at[trip, back],
            device_id=(tx, ty), device_id_type=MESH)

    def near_arrival(trip, slot):
        here = strip_in.at[trip, slot] if slot < 4 else corner_in.at[trip, slot - 4]
        return pltpu.make_async_copy(here, here, near_recv.at[trip, slot])

    def seam_copy(trip, which, step, tx, ty):
        slot = rims[which][4]
        line = seam[trip].at[slot, 0:faces] if trip == 0 else seam[trip].at[slot]
        return pltpu.make_async_remote_copy(
            src_ref=line, dst_ref=line, send_sem=seam_send.at[trip, which, step],
            recv_sem=seam_recv.at[trip], device_id=(tx, ty), device_id_type=MESH)

    def end_copy(trip, which, end):
        active, edge, place, count, slot = rims[which]
        spot = place + 2 * end - 1
        if which == 0:
            tx, ty, back = x, spot, 2 * edge + 1 - end
        else:
            tx, ty, back = spot, y, edge - 2 + 2 * (1 - end)
        return pltpu.make_async_remote_copy(
            src_ref=end_src.at[trip, which, end], dst_ref=corner_in.at[trip, back],
            send_sem=ends_send.at[trip, which, end], recv_sem=near_recv.at[trip, 4 + back],
            device_id=(tx, ty), device_id_type=MESH)

    def send_all(trip):
        for which in range(2):
            for step, tx, ty, on in partners(which):
                @pl.when(on)
                def _(which=which, step=step, tx=tx, ty=ty):
                    seam_copy(trip, which, step, tx, ty).start()
        for item in near:
            @pl.when(item[2])
            def _(item=item):
                near_copy(trip, item).start()

    def wait_sent(trip):
        for which in range(2):
            for step, tx, ty, on in partners(which):
                @pl.when(on)
                def _(which=which, step=step, tx=tx, ty=ty):
                    seam_copy(trip, which, step, tx, ty).wait_send()
            active, edge, place, count, slot = rims[which]
            for end in range(2):
                @pl.when(jnp.logical_and(active, place < count - 1 if end else place > 0))
                def _(which=which, end=end):
                    end_copy(trip, which, end).wait_send()
        for item in near:
            @pl.when(item[2])
            def _(item=item):
                near_copy(trip, item).wait_send()

    first_last = jnp.where(
        jnp.logical_and(
            cols_iota((32, strip)) == (rows_iota((32, strip)) % 16) * side + (rows_iota((32, strip)) // 16) * (side - 1),
            rows_iota((32, strip)) % 16 < faces),
        1.0, 0.0).astype(BF16)

    def own_lines(trip):
        for which in range(2):
            active, edge, place, count, slot = rims[which]

            @pl.when(active)
            def _(which=which, edge=edge, slot=slot):
                seam[trip][slot, 0:faces] = src[trip, edge]
                if trip == 1:
                    for end in range(2):
                        at = 2 * edge + end if which == 0 else edge - 2 + 2 * end
                        seam[trip][slot, faces + end] = corner_src[trip, at]

    def prepare_choice():
        for which in range(2):
            active, edge, place, count, slot = rims[which]

            @pl.when(active)
            def _(which=which, edge=edge, place=place, count=count):
                row, col = rows_iota((strip, strip)), cols_iota((strip, strip))
                mirrored = row - 2 * (row % side) + (side - 1)
                end_row, end_col = rows_iota((16, 256)), cols_iota((16, 256))
                wanted = row
                chosen = [jnp.zeros((16, 256), F32)] * 2
                for f in range(faces):
                    flip = flip_tab[edge, f]
                    flipped = jnp.logical_and(row // side == f, jnp.full((strip, strip), flip, jnp.int32) == 1)
                    wanted = jnp.where(flipped, mirrored, wanted)
                    part = place // (count // 2)
                    part = part + flip * (1 - 2 * part)
                    for end in range(2):
                        code = ((part * 4 + edge_tab[edge, f]) * 2 + end + flip * (1 - 2 * end)) * 16 + face_tab[edge, f]
                        hit = jnp.logical_and(end_row == f, end_col == code)
                        chosen[end] = jnp.where(hit, 1.0, chosen[end])
                turner[which] = jnp.where(wanted == col, 1.0, 0.0).astype(BF16)
                for end in range(2):
                    chooser[which, end] = chosen[end].astype(BF16)

    def strip_arrivals(trip):
        @pl.when(rim)
        def _():
            @pl.when(corner)
            def _():
                here = seam[trip].at[0:6, 0:faces] if trip == 0 else seam[trip].at[0:6]
                pltpu.make_async_copy(here, here, seam_recv.at[trip]).wait()

            @pl.when(jnp.logical_not(corner))
            def _():
                here = seam[trip].at[0:7, 0:faces] if trip == 0 else seam[trip].at[0:7]
                pltpu.make_async_copy(here, here, seam_recv.at[trip]).wait()
        for which in range(2):
            active, edge, place, count, slot = rims[which]

            @pl.when(active)
            def _(which=which, edge=edge, place=place, count=count):
                part = place // (count // 2)
                lines = []
                for f in range(faces):
                    flip = flip_tab[edge, f]
                    lines.append(seam[trip][(part + flip * (1 - 2 * part)) * 4 + edge_tab[edge, f], face_tab[edge, f]])
                line = dot(turner[which], jnp.concatenate(lines, axis=0)).astype(BF16)
                strip_in[trip, edge] = line.reshape(faces, side, width)
                if trip == 0:
                    picked = dot(first_last, line).astype(BF16)
                    ends = [picked[:16], picked[16:]]
                else:
                    offered = jnp.concatenate(
                        [seam[trip][slot, faces + end] for slot in range(8) for end in range(2)], axis=0)
                    ends = [dot(chooser[which, end], offered).astype(BF16) for end in range(2)]
                for end in range(2):
                    end_src[trip, which, end] = ends[end]

                    @pl.when(place < count - 1 if end else place > 0)
                    def _(end=end):
                        end_copy(trip, which, end).start()
        for item in near:
            if item[3] < 4:
                @pl.when(item[2])
                def _(item=item):
                    near_arrival(trip, item[3]).wait()

    def corner_arrivals(trip):
        for v in range(2):
            for h in range(2):
                both = jnp.logical_and(bottom if v else top, right if h else left)

                @pl.when(jnp.logical_not(both))
                def _(v=v, h=h):
                    near_arrival(trip, 4 + 2 * v + h).wait()

                @pl.when(both)
                def _(v=v, h=h):
                    if trip == 0:
                        total = end_src[0, 0, h].astype(F32) + end_src[0, 1, v].astype(F32)
                        corner_in[0, 2 * v + h] = (0.5 * total).astype(BF16)
                    else:
                        corner_in[1, 2 * v + h] = jnp.zeros((16, width), BF16)

    load_x = pltpu.make_async_copy(x_hbm, xp.at[:, 1:side + 1], load_sem.at[0])
    load_w = pltpu.make_async_copy(w_hbm, w9, load_sem.at[1])
    load_c = pltpu.make_async_copy(cot_hbm, cot, load_sem.at[2])
    loads = [pltpu.make_async_copy(there, here, load_sem.at[3 + i]) for i, (there, here) in enumerate(
        ((face_hbm, face_tab), (edge_hbm, edge_tab), (flip_hbm, flip_tab), (bias_hbm, bias_ref)))]
    load_x.start()
    load_w.start()
    for load in loads:
        load.start()
    load_c.start()

    barrier = pltpu.get_barrier_semaphore()
    due = jnp.int32(0)

    def greet(on, tx, ty):
        @pl.when(on)
        def _():
            pl.semaphore_signal(barrier, inc=1, device_id=(tx, ty), device_id_type=MESH)
        return on.astype(jnp.int32)

    for which in range(2):
        for step, tx, ty, on in partners(which):
            due = due + greet(jnp.logical_and(on, jnp.logical_not(corner)) if which else on, tx, ty)
    for tx, ty, inside, slot, back in near:
        due = due + greet(inside, tx, ty)

    zero_rows = jnp.zeros((faces, side, width), BF16)
    xp[:, 0] = zero_rows
    xp[:, side + 1] = zero_rows
    sp[:, 0] = zero_rows
    sp[:, side + 1] = zero_rows
    load_x.wait()
    src[0, 0] = xp[:, 1]
    src[0, 1] = xp[:, side]
    column_pick = jnp.where(
        cols_iota((2 * side, cells)) == (rows_iota((2 * side, cells)) % side) * side
        + (rows_iota((2 * side, cells)) // side) * (side - 1), 1.0, 0.0).astype(BF16)
    for f in range(faces):
        both = dot(column_pick, xp[f, 1:side + 1].reshape(cells, width)).astype(BF16)
        src[0, 2, f] = both[:side]
        src[0, 3, f] = both[side:]
    for half in range(2):
        picked = dot(first_last, src[0, half].reshape(strip, width)).astype(BF16)
        corner_src[0, 2 * half] = picked[:16]
        corner_src[0, 2 * half + 1] = picked[16:]
    own_lines(0)
    pl.semaphore_wait(barrier, due)
    send_all(0)

    load_w.wait()
    for a in range(3):
        for b in range(3):
            tap = w9[a, b]
            back = tap.astype(F32).T.astype(BF16)
            wf[a * width:(a + 1) * width, b * width:(b + 1) * width] = tap
            vf[(2 - a) * width:(3 - a) * width, (2 - b) * width:(3 - b) * width] = back
            if b != 1:
                wcol[b // 2, :, a * width:(a + 1) * width] = tap
                vcol[b // 2, :, (2 - a) * width:(3 - a) * width] = back
    for load in loads:
        load.wait()
    prepare_choice()
    load_c.wait()
    for f in range(faces):
        both = dot(column_pick, cot[f].reshape(cells, width))
        colcot[0, f * side:(f + 1) * side] = both[:side]
        colcot[1, f * side:(f + 1) * side] = both[side:]

    def conv(source, f, weights):
        stacked = jnp.concatenate(
            [source[f, a:a + side].reshape(cells, width) for a in range(3)], axis=1)
        return shifted_sum(dot(stacked, weights), side)

    def forward_face(f, carry):
        acc[pl.ds(pl.multiple_of(f * cells, cells), cells)] = conv(xp, f, wf[...]) + bias_ref[...]
        return carry
    lax.fori_loop(0, faces, forward_face, 0)

    def add_strips(strips):
        for half in range(2):
            line = strips[half]
            for f in range(faces):
                at = f * cells + half * (cells - side)
                acc[at:at + side] += line[f * side:(f + 1) * side]
        for half in range(2):
            at = pl.ds(half * (side - 1), strip, stride=side)
            acc[at] = acc[at] + strips[2 + half]

    def add_corners(corners):
        for which in range(4):
            at = pl.ds((which // 2) * (cells - side) + (which % 2) * (side - 1), faces, stride=cells)
            acc[at] = acc[at] + corners[which]

    strip_arrivals(0)
    strips = []
    for edge in range(4):
        line = strip_in[0, edge].reshape(strip, width)
        weights = wf[2 * edge * width:(2 * edge + 1) * width] if edge < 2 else wcol[edge - 2]
        strips.append(shifted_sum(dot(line, weights), side))
    add_strips(strips)
    corner_arrivals(0)
    add_corners([dot(corner_in[0, 2 * a + b], w9[2 * a, 2 * b])[:faces] for a in range(2) for b in range(2)])

    rim_slopes = []
    for half in range(2):
        at = half * (cells - side)
        line = jnp.concatenate([acc[f * cells + at:f * cells + at + side] for f in range(faces)], axis=0)
        rim_slopes.append((cot[:, half * (side - 1)].reshape(strip, width).astype(F32) * silu_parts(line)[1]).astype(BF16))
    for half in range(2):
        line = acc[pl.ds(half * (side - 1), strip, stride=side)]
        rim_slopes.append((colcot[half] * silu_parts(line)[1]).astype(BF16))
    for edge in range(4):
        weights = vf[2 * (1 - edge) * width:(2 * (1 - edge) + 1) * width] if edge < 2 else vcol[edge - 2]
        ring[edge] = shifted_sum(dot(rim_slopes[edge], weights), side)
    for a in range(2):
        picked = dot(first_last, rim_slopes[a]).astype(BF16)
        for b in range(2):
            beyond = dot(picked[16 * b:16 * b + 16], vf[2 * (1 - a) * width:(2 * (1 - a) + 1) * width,
                                                        2 * (1 - b) * width:(2 * (1 - b) + 1) * width])
            corner_src[1, 2 * a + b] = beyond.astype(BF16)

            @pl.when(jnp.logical_and(bottom if a else top, right if b else left))
            def _(a=a, b=b, beyond=beyond):
                along_row = pl.ds(b * (side - 1), faces, stride=side)
                along_col = pl.ds(a * (side - 1), faces, stride=side)
                ring[a, along_row] = ring[a, along_row] + 0.5 * beyond[:faces]
                ring[2 + b, along_col] = ring[2 + b, along_col] + 0.5 * beyond[:faces]
    for edge in range(4):
        src[1, edge] = ring[edge].astype(BF16).reshape(faces, side, width)
    own_lines(1)
    send_all(1)

    def adjoint_face(f, carry):
        at = pl.ds(pl.multiple_of(f * cells, cells), cells)
        value, slope = silu_parts(acc[at])
        act[f] = value.astype(BF16).reshape(side, side, width)
        slope = cot[f].reshape(cells, width).astype(F32) * slope
        sp[f, 1:side + 1] = slope.astype(BF16).reshape(side, side, width)
        acc[at] = conv(sp, f, vf[...])
        return carry
    lax.fori_loop(0, faces, adjoint_face, 0)

    strip_arrivals(1)
    add_strips([strip_in[1, edge].reshape(strip, width).astype(F32) for edge in range(4)])
    corner_arrivals(1)
    add_corners([corner_in[1, which].astype(F32)[:faces] for which in range(4)])

    def finish_face(f, carry):
        at = pl.ds(pl.multiple_of(f * cells, cells), cells)
        grad[f] = acc[at].astype(BF16).reshape(side, side, width)
        return carry
    lax.fori_loop(0, faces, finish_face, 0)
    wait_sent(0)
    wait_sent(1)


def shards(features, weight, out_bias, cotangent, seam_face, seam_edge, seam_flip):
    faces, side, _, width = features.shape
    nx, ny = lax.axis_size("fx"), lax.axis_size("fy")
    patch = (faces, side, side, width)
    padded = (faces, side + 2, side, width)
    strip = faces * side
    dma = pltpu.SemaphoreType.DMA
    hbm = pl.BlockSpec(memory_space=pltpu.HBM)
    vmem = pl.BlockSpec(memory_space=pltpu.VMEM)
    return pl.pallas_call(
        functools.partial(kernel, nx, ny, faces, side, width),
        out_shape=(jax.ShapeDtypeStruct(patch, BF16), jax.ShapeDtypeStruct(patch, BF16)),
        in_specs=[hbm] * 7,
        out_specs=(vmem, vmem),
        scratch_shapes=[
            pltpu.SMEM((4, faces), jnp.int32),
            pltpu.SMEM((4, faces), jnp.int32),
            pltpu.SMEM((4, faces), jnp.int32),
            pltpu.VMEM((1, width), F32),
            pltpu.VMEM(padded, BF16),
            pltpu.VMEM(patch, BF16),
            pltpu.VMEM((3, 3, width, width), BF16),
            pltpu.VMEM((faces * side * side, width), F32),
            pltpu.VMEM(padded, BF16),
            pltpu.VMEM((3 * width, 3 * width), BF16),
            pltpu.VMEM((2, width, 3 * width), BF16),
            pltpu.VMEM((3 * width, 3 * width), BF16),
            pltpu.VMEM((2, width, 3 * width), BF16),
            pltpu.VMEM((2, strip, width), F32),
            pltpu.VMEM((4, strip, width), F32),
            pltpu.VMEM((2, strip, strip), BF16),
            pltpu.VMEM((2, 2, 16, 256), BF16),
            pltpu.VMEM((2, 4, faces, side, width), BF16),
            pltpu.VMEM((2, 4, 16, width), BF16),
            pltpu.VMEM((2, 4, faces, side, width), BF16),
            pltpu.VMEM((2, 4, 16, width), BF16),
            pltpu.VMEM((8, faces + 2, side, width), BF16),
            pltpu.VMEM((8, faces + 2, side, width), BF16),
            pltpu.VMEM((2, 2, 2, 16, width), BF16),
            dma((2, 8)),
            dma((2, 8)),
            dma((2, 2, 8)),
            dma((2,)),
            dma((2, 2, 2)),
            dma((7,)),
        ],
        compiler_params=pltpu.CompilerParams(
            collective_id=0, has_side_effects=True, vmem_limit_bytes=40 * 1024 * 1024),
    )(*[pltpu.with_memory_space_constraint(value, pltpu.HBM) for value in (
        seam_face.T, seam_edge.T, seam_flip.T, out_bias.reshape(1, width), features, weight, cotangent)])


def solution(mesh):
    in_specs = (P(None, "fx", "fy", None), P(), P(), P(None, "fx", "fy", None), P(), P(), P())
    out_specs = (P(None, "fx", "fy", None), P(None, "fx", "fy", None))
    return jax.shard_map(shards, mesh=mesh, in_specs=in_specs, out_specs=out_specs, check_vma=False)
```

```python
import functools

import jax
import jax.numpy as jnp
from jax import lax
from jax.experimental import pallas as pl
from jax.experimental.pallas import tpu as pltpu
from jax.sharding import PartitionSpec as P

MESH = pl.DeviceIdType.MESH
F32 = jnp.float32
BF16 = jnp.bfloat16


def dot(a, b):
    return jnp.dot(a, b, preferred_element_type=F32)


def rows_iota(shape):
    return lax.broadcasted_iota(jnp.int32, shape, 0)


def cols_iota(shape):
    return lax.broadcasted_iota(jnp.int32, shape, 1)


def shifted_sum(taps, run):
    total, width = taps.shape[0], taps.shape[1] // 3
    place = rows_iota((total, width)) % run
    below = jnp.where(place == 0, 0.0, pltpu.roll(taps[:, :width], 1, 0))
    above = jnp.where(place == run - 1, 0.0, pltpu.roll(taps[:, 2 * width:], total - 1, 0))
    return taps[:, width:2 * width] + below + above


def silu_parts(value):
    sigma = 1.0 / (1.0 + jnp.exp(-value))
    return value * sigma, sigma * (1.0 + value * (1.0 - sigma))


def kernel(nx, ny, faces, side, width,
           face_hbm, edge_hbm, flip_hbm, bias_hbm, x_hbm, w_hbm, cot_hbm,
           act, grad,
           face_tab, edge_tab, flip_tab, bias_ref, xp, cot, w9, acc, sp,
           wf, wcol, vf, vcol, colcot, ring, turner, chooser, end_cells,
           src, corner_src, strip_in, corner_in, seam_first, seam_second,
           near_send, near_recv, seam_send, seam_recv, tail_send, relay_send, ends_send, ends_recv, load_sem):
    x = lax.axis_index("fx")
    y = lax.axis_index("fy")
    top, bottom, left, right = x == 0, x == nx - 1, y == 0, y == ny - 1
    on_rim = (top, bottom, left, right)
    row_rim = jnp.logical_or(top, bottom)
    col_rim = jnp.logical_or(left, right)
    rim = jnp.logical_or(row_rim, col_rim)
    corner = jnp.logical_and(row_rim, col_rim)
    seam = (seam_first, seam_second)
    cells = side * side
    strip = faces * side
    last_row = cells - side
    row_edge = x // (nx - 1)
    col_edge = 2 + y // (ny - 1)
    rims = ((row_rim, row_edge, y, ny, (y // (ny // 2)) * 4 + row_edge),
            (col_rim, col_edge, x, nx, (x // (nx // 2)) * 4 + col_edge))

    near = []
    for dx, dy, slot in ((-1, 0, 0), (1, 0, 1), (0, -1, 2), (0, 1, 3), (-1, -1, 4), (-1, 1, 5), (1, -1, 6), (1, 1, 7)):
        tx, ty = x + dx, y + dy
        inside = None
        for ok in ([tx >= 0] if dx < 0 else [tx < nx] if dx > 0 else []) + ([ty >= 0] if dy < 0 else [ty < ny] if dy > 0 else []):
            inside = ok if inside is None else jnp.logical_and(inside, ok)
        back = slot ^ 1 if slot < 4 else 4 + (3 - (slot - 4))
        near.append((tx, ty, inside, slot, back))

    def partners(which, tail=True):
        active, edge, place, count, slot = rims[which]
        for kind in range(2):
            for half in range(2):
                for turn in range(2):
                    spot = count - 1 - place if turn else place
                    tx, ty = (half * (nx - 1), spot) if kind == 0 else (spot, half * (ny - 1))
                    other = jnp.logical_not(jnp.logical_and(tx == x, ty == y))
                    on = jnp.logical_and(active, other)
                    if kind == 1:
                        on = jnp.logical_and(on, jnp.logical_not(corner))
                    by_relay = which == 0 and kind == 0 and turn == 1
                    if by_relay and not tail:
                        on = jnp.logical_and(on, jnp.logical_or(corner, half == row_edge))
                    yield kind * 4 + half * 2 + turn, tx, ty, on

    def near_copy(trip, item):
        tx, ty, inside, slot, back = item
        if slot < 4:
            source, target = src.at[trip, slot], strip_in.at[trip, back]
        else:
            source, target = corner_src.at[trip, slot - 4], corner_in.at[trip, back - 4]
        return pltpu.make_async_remote_copy(
            src_ref=source, dst_ref=target, send_sem=near_send.at[trip, slot], recv_sem=near_recv.at[trip, back],
            device_id=(tx, ty), device_id_type=MESH)

    def near_arrival(trip, slot):
        here = strip_in.at[trip, slot] if slot < 4 else corner_in.at[trip, slot - 4]
        return pltpu.make_async_copy(here, here, near_recv.at[trip, slot])

    def end_spot(which, edge, end):
        return 2 * edge + end if which == 0 else edge - 2 + 2 * end

    def has_next(which, end):
        place, count = rims[which][2], rims[which][3]
        return place < count - 1 if end else place > 0

    def seam_copy(trip, which, step, tx, ty, tail):
        slot = rims[which][4]
        line = seam[trip].at[slot, faces:faces + 2] if tail else seam[trip].at[slot, 0:faces]
        sems = tail_send if tail else seam_send
        straight = which == 0 and not tail and step < 4 and step % 2 == 0
        arrived = seam_recv.at[trip, 1 if tail else 0]
        if straight:
            arrived = seam_recv.at[trip, 2 * jnp.logical_not(corner).astype(jnp.int32)]
        return pltpu.make_async_remote_copy(
            src_ref=line, dst_ref=line, send_sem=sems.at[trip, which, step],
            recv_sem=arrived, device_id=(tx, ty), device_id_type=MESH)

    relays = jnp.logical_and(row_rim, jnp.logical_not(corner))

    def relay_line(trip):
        return seam[trip].at[(y // (ny // 2)) * 4 + 1 - row_edge, 0:faces]

    def relay_copy(trip):
        line = relay_line(trip)
        return pltpu.make_async_remote_copy(
            src_ref=line, dst_ref=line, send_sem=relay_send.at[trip],
            recv_sem=seam_recv.at[trip, 0], device_id=(x, ny - 1 - y), device_id_type=MESH)

    def send_relay(trip):
        @pl.when(relays)
        def _():
            line = relay_line(trip)
            pltpu.make_async_copy(line, line, seam_recv.at[trip, 2]).wait()
            relay_copy(trip).start()

    def end_copy(trip, which, end):
        active, edge, place, count, slot = rims[which]
        spot = place + 2 * end - 1
        tx, ty = (x, spot) if which == 0 else (spot, y)
        return pltpu.make_async_remote_copy(
            src_ref=corner_src.at[trip, end_spot(which, edge, end)],
            dst_ref=seam[trip].at[(spot // (count // 2)) * 4 + edge, faces + 1 - end],
            send_sem=ends_send.at[trip, which, end], recv_sem=ends_recv.at[trip, which, 1 - end],
            device_id=(tx, ty), device_id_type=MESH)

    def send_line(trip, which):
        active = rims[which][0]
        for end in range(2):
            @pl.when(jnp.logical_and(active, has_next(which, end)))
            def _(end=end):
                end_copy(trip, which, end).start()
        for step, tx, ty, on in partners(which, False):
            @pl.when(on)
            def _(step=step, tx=tx, ty=ty):
                seam_copy(trip, which, step, tx, ty, False).start()

    def send_tails(trip):
        for which in range(2):
            active, edge, place, count, slot = rims[which]
            for end in range(2):
                @pl.when(jnp.logical_and(active, has_next(which, end)))
                def _(which=which, end=end, slot=slot):
                    here = seam[trip].at[slot, faces + end]
                    pltpu.make_async_copy(here, here, ends_recv.at[trip, which, end]).wait()
            for step, tx, ty, on in partners(which):
                @pl.when(on)
                def _(which=which, step=step, tx=tx, ty=ty):
                    seam_copy(trip, which, step, tx, ty, True).start()

    def send_near(trip, slots):
        for item in near:
            if item[3] in slots:
                @pl.when(item[2])
                def _(item=item):
                    near_copy(trip, item).start()

    def wait_sent(trip):
        @pl.when(rim)
        def _():
            for which in range(2):
                active = rims[which][0]
                for step, tx, ty, on in partners(which, False):
                    @pl.when(on)
                    def _(which=which, step=step, tx=tx, ty=ty):
                        seam_copy(trip, which, step, tx, ty, False).wait_send()
                for step, tx, ty, on in partners(which):
                    @pl.when(on)
                    def _(which=which, step=step, tx=tx, ty=ty):
                        seam_copy(trip, which, step, tx, ty, True).wait_send()
                for end in range(2):
                    @pl.when(jnp.logical_and(active, has_next(which, end)))
                    def _(which=which, end=end):
                        end_copy(trip, which, end).wait_send()
        @pl.when(relays)
        def _():
            relay_copy(trip).wait_send()
        for item in near:
            @pl.when(item[2])
            def _(item=item):
                near_copy(trip, item).wait_send()

    first_last = jnp.where(
        jnp.logical_and(
            cols_iota((32, strip)) == (rows_iota((32, strip)) % 16) * side + (rows_iota((32, strip)) // 16) * (side - 1),
            rows_iota((32, strip)) % 16 < faces),
        1.0, 0.0).astype(BF16)

    def prepare_choice():
        for which in range(2):
            active, edge, place, count, slot = rims[which]

            @pl.when(active)
            def _(which=which, edge=edge, place=place, count=count):
                row, col = rows_iota((strip, strip)), cols_iota((strip, strip))
                mirrored = row - 2 * (row % side) + (side - 1)
                end_row, end_col = rows_iota((16, 256)), cols_iota((16, 256))
                wanted = row
                chosen = [jnp.zeros((16, 256), F32)] * 2
                for f in range(faces):
                    flip = flip_tab[edge, f]
                    flipped = jnp.logical_and(row // side == f, jnp.full((strip, strip), flip, jnp.int32) == 1)
                    wanted = jnp.where(flipped, mirrored, wanted)
                    part = place // (count // 2)
                    part = part + flip * (1 - 2 * part)
                    for end in range(2):
                        code = ((part * 4 + edge_tab[edge, f]) * 2 + end + flip * (1 - 2 * end)) * 16 + face_tab[edge, f]
                        hit = jnp.logical_and(end_row == f, end_col == code)
                        chosen[end] = jnp.where(hit, 1.0, chosen[end])
                turner[which] = jnp.where(wanted == col, 1.0, 0.0).astype(BF16)
                for end in range(2):
                    chooser[which, end] = chosen[end].astype(BF16)

    def seam_arrivals(trip):
        def wait_for(lines, tails):
            here = seam[trip].at[0:lines, 0:faces]
            pltpu.make_async_copy(here, here, seam_recv.at[trip, 0]).wait()
            here = seam[trip].at[0:tails, 0:2]
            pltpu.make_async_copy(here, here, seam_recv.at[trip, 1]).wait()

        @pl.when(corner)
        def _():
            wait_for(6, 6)

        @pl.when(relays)
        def _():
            wait_for(6, 7)

        @pl.when(jnp.logical_not(row_rim))
        def _():
            wait_for(7, 7)
        for which in range(2):
            active, edge, place, count, slot = rims[which]

            @pl.when(active)
            def _(which=which, edge=edge, place=place, count=count):
                part = place // (count // 2)
                lines = []
                for f in range(faces):
                    flip = flip_tab[edge, f]
                    lines.append(seam[trip][(part + flip * (1 - 2 * part)) * 4 + edge_tab[edge, f], face_tab[edge, f]])
                line = dot(turner[which], jnp.concatenate(lines, axis=0)).astype(BF16)
                strip_in[trip, edge] = line.reshape(faces, side, width)
                if trip == 0:
                    @pl.when(corner)
                    def _():
                        end_cells[which] = dot(first_last, line)
                offered = jnp.concatenate(
                    [seam[trip][slot, faces + end] for slot in range(8) for end in range(2)], axis=0)
                for end in range(2):
                    value = dot(chooser[which, end], offered).astype(BF16)

                    @pl.when(has_next(which, end))
                    def _(end=end, value=value):
                        corner_in[trip, end_spot(which, edge, end)] = value

    load_x = pltpu.make_async_copy(x_hbm, xp.at[:, 1:side + 1], load_sem.at[0])
    load_w = pltpu.make_async_copy(w_hbm, w9, load_sem.at[1])
    load_c = pltpu.make_async_copy(cot_hbm, cot, load_sem.at[2])
    loads = [pltpu.make_async_copy(there, here, load_sem.at[3 + i]) for i, (there, here) in enumerate(
        ((face_hbm, face_tab), (edge_hbm, edge_tab), (flip_hbm, flip_tab), (bias_hbm, bias_ref)))]
    load_x.start()
    load_w.start()
    for load in loads:
        load.start()
    load_c.start()

    barrier = pltpu.get_barrier_semaphore()
    due = jnp.int32(0)

    def greet(on, tx, ty):
        @pl.when(on)
        def _():
            pl.semaphore_signal(barrier, inc=1, device_id=(tx, ty), device_id_type=MESH)
        return on.astype(jnp.int32)

    for which in range(2):
        for step, tx, ty, on in partners(which):
            due = due + greet(jnp.logical_and(on, jnp.logical_not(corner)) if which else on, tx, ty)
    for tx, ty, inside, slot, back in near:
        due = due + greet(inside, tx, ty)

    zero_rows = jnp.zeros((faces, side, width), BF16)
    zero_tile = jnp.zeros((side, width), BF16)
    xp[:, 0] = zero_rows
    xp[:, side + 1] = zero_rows
    sp[:, 0] = zero_rows
    sp[:, side + 1] = zero_rows
    for which in range(2):
        for end in range(2):
            @pl.when(jnp.logical_and(rims[which][0], jnp.logical_not(has_next(which, end))))
            def _(which=which, end=end):
                for trip in range(2):
                    seam[trip][rims[which][4], faces + end] = zero_tile
    load_x.wait()
    for half in range(2):
        line = xp[:, 1 + half * (side - 1)]
        src[0, half] = line
        picked = dot(first_last, line.reshape(strip, width)).astype(BF16)
        corner_src[0, 2 * half] = picked[:16]
        corner_src[0, 2 * half + 1] = picked[16:]

        @pl.when(on_rim[half])
        def _(line=line):
            seam[0][rims[0][4], 0:faces] = line
    pl.semaphore_wait(barrier, due)
    send_line(0, 0)
    send_near(0, (0, 1, 4, 5, 6, 7))
    column_pick = jnp.where(
        cols_iota((2 * side, cells)) == (rows_iota((2 * side, cells)) % side) * side
        + (rows_iota((2 * side, cells)) // side) * (side - 1), 1.0, 0.0).astype(BF16)
    for f in range(faces):
        both = dot(column_pick, xp[f, 1:side + 1].reshape(cells, width)).astype(BF16)
        src[0, 2, f] = both[:side]
        src[0, 3, f] = both[side:]

    @pl.when(col_rim)
    def _():
        seam[0][rims[1][4], 0:faces] = src[0, col_edge]
    send_line(0, 1)
    send_near(0, (2, 3))
    send_tails(0)
    send_relay(0)

    load_w.wait()
    for a in range(3):
        for b in range(3):
            tap = w9[a, b]
            back = tap.astype(F32).T.astype(BF16)
            wf[a * width:(a + 1) * width, b * width:(b + 1) * width] = tap
            vf[(2 - a) * width:(3 - a) * width, (2 - b) * width:(3 - b) * width] = back
            if b != 1:
                wcol[b // 2, :, a * width:(a + 1) * width] = tap
                vcol[b // 2, :, (2 - a) * width:(3 - a) * width] = back
    for load in loads:
        load.wait()
    prepare_choice()
    load_c.wait()
    for f in range(faces):
        both = dot(column_pick, cot[f].reshape(cells, width))
        colcot[0, f * side:(f + 1) * side] = both[:side]
        colcot[1, f * side:(f + 1) * side] = both[side:]

    def conv(source, f, weights):
        stacked = jnp.concatenate(
            [source[f, a:a + side].reshape(cells, width) for a in range(3)], axis=1)
        return shifted_sum(dot(stacked, weights), side)

    def forward_face(f, carry):
        acc[pl.ds(pl.multiple_of(f * cells, cells), cells)] = conv(xp, f, wf[...]) + bias_ref[...]
        return carry
    lax.fori_loop(0, faces, forward_face, 0)

    def add_strip(edge, value):
        if edge < 2:
            for f in range(faces):
                at = f * cells + edge * last_row
                acc[at:at + side] += value[f * side:(f + 1) * side]
        else:
            at = pl.ds((edge - 2) * (side - 1), strip, stride=side)
            acc[at] = acc[at] + value

    def corner_at(v, h):
        return pl.ds(v * last_row + h * (side - 1), faces, stride=cells)

    def add_corner(v, h, value):
        acc[corner_at(v, h)] = acc[corner_at(v, h)] + value

    def forward_strip(edge):
        line = strip_in[0, edge].reshape(strip, width)
        weights = wf[2 * edge * width:(2 * edge + 1) * width] if edge < 2 else wcol[edge - 2]
        add_strip(edge, shifted_sum(dot(line, weights), side))

    def forward_corner(v, h):
        add_corner(v, h, dot(corner_in[0, 2 * v + h], w9[2 * v, 2 * h])[:faces])

    def from_near(trip, strip_step, corner_step):
        for item in near:
            @pl.when(item[2])
            def _(item=item):
                near_arrival(trip, item[3]).wait()
                if item[3] < 4:
                    strip_step(item[3])
                else:
                    corner_step((item[3] - 4) // 2, item[3] % 2)

    corner_pairs = [(v, h) for v in range(2) for h in range(2)]

    def at_both(v, h):
        return jnp.logical_and(bottom if v else top, right if h else left)

    from_near(0, forward_strip, forward_corner)

    @pl.when(rim)
    def _():
        seam_arrivals(0)
        for v, h in corner_pairs:
            @pl.when(at_both(v, h))
            def _(v=v, h=h):
                total = end_cells[0, 16 * h:16 * h + 16] + end_cells[1, 16 * v:16 * v + 16]
                corner_in[0, 2 * v + h] = (0.5 * total).astype(BF16)
        for edge in range(4):
            @pl.when(on_rim[edge])
            def _(edge=edge):
                forward_strip(edge)
        for v, h in corner_pairs:
            @pl.when(jnp.logical_or(bottom if v else top, right if h else left))
            def _(v=v, h=h):
                forward_corner(v, h)

    def ring_strip(edge):
        if edge < 2:
            at = edge * last_row
            line = jnp.concatenate([acc[f * cells + at:f * cells + at + side] for f in range(faces)], axis=0)
            turned_cot = cot[:, edge * (side - 1)].reshape(strip, width).astype(F32)
            weights = vf[2 * (1 - edge) * width:(2 * (1 - edge) + 1) * width]
        else:
            line = acc[pl.ds((edge - 2) * (side - 1), strip, stride=side)]
            turned_cot = colcot[edge - 2]
            weights = vcol[edge - 2]
        slope = (turned_cot * silu_parts(line)[1]).astype(BF16)
        return shifted_sum(dot(slope, weights), side)

    beyond = []
    for v, h in corner_pairs:
        slope = colcot.at[h][pl.ds(v * (side - 1), faces, stride=side)] * silu_parts(acc[corner_at(v, h)])[1]
        slope = jnp.concatenate([slope, jnp.zeros((16 - faces, width), F32)], axis=0).astype(BF16)
        value = dot(slope, vf[2 * (1 - v) * width:(2 * (1 - v) + 1) * width, 2 * (1 - h) * width:(2 * (1 - h) + 1) * width])
        beyond.append(value)
        corner_src[1, 2 * v + h] = value.astype(BF16)

    @pl.when(rim)
    def _():
        for edge in range(4):
            @pl.when(on_rim[edge])
            def _(edge=edge):
                ring[edge] = ring_strip(edge)
        for v, h in corner_pairs:
            @pl.when(at_both(v, h))
            def _(v=v, h=h):
                along_row = pl.ds(h * (side - 1), faces, stride=side)
                along_col = pl.ds(v * (side - 1), faces, stride=side)
                ring[v, along_row] = ring[v, along_row] + 0.5 * beyond[2 * v + h][:faces]
                ring[2 + h, along_col] = ring[2 + h, along_col] + 0.5 * beyond[2 * v + h][:faces]
        for which in range(2):
            active, edge, place, count, slot = rims[which]

            @pl.when(active)
            def _(edge=edge, slot=slot):
                seam[1][slot, 0:faces] = ring[edge].astype(BF16).reshape(faces, side, width)
            send_line(1, which)
    for edge in range(4):
        @pl.when(jnp.logical_not(on_rim[edge]))
        def _(edge=edge):
            src[1, edge] = ring_strip(edge).astype(BF16).reshape(faces, side, width)
    send_near(1, range(8))
    send_tails(1)
    send_relay(1)

    def adjoint_face(f, carry):
        at = pl.ds(pl.multiple_of(f * cells, cells), cells)
        value, slope = silu_parts(acc[at])
        act[f] = value.astype(BF16).reshape(side, side, width)
        slope = cot[f].reshape(cells, width).astype(F32) * slope
        sp[f, 1:side + 1] = slope.astype(BF16).reshape(side, side, width)
        acc[at] = conv(sp, f, vf[...])
        return carry
    lax.fori_loop(0, faces, adjoint_face, 0)

    def adjoint_strip(edge):
        add_strip(edge, strip_in[1, edge].reshape(strip, width).astype(F32))

    def adjoint_corner(v, h):
        add_corner(v, h, corner_in[1, 2 * v + h].astype(F32)[:faces])

    def finish_face(f, carry):
        at = pl.ds(pl.multiple_of(f * cells, cells), cells)
        grad[f] = acc[at].astype(BF16).reshape(side, side, width)
        return carry

    wait_sent(0)
    from_near(1, adjoint_strip, adjoint_corner)

    @pl.when(jnp.logical_not(col_rim))
    def _():
        lax.fori_loop(0, faces, finish_face, 0)
    wait_sent(1)

    @pl.when(rim)
    def _():
        seam_arrivals(1)
        for edge in range(4):
            @pl.when(on_rim[edge])
            def _(edge=edge):
                adjoint_strip(edge)
        for v, h in corner_pairs:
            vertical, horizontal = bottom if v else top, right if h else left

            @pl.when(vertical != horizontal)
            def _(v=v, h=h):
                adjoint_corner(v, h)

        @pl.when(col_rim)
        def _():
            lax.fori_loop(0, faces, finish_face, 0)
        for edge in range(2):
            @pl.when(jnp.logical_and(on_rim[edge], jnp.logical_not(col_rim)))
            def _(edge=edge):
                for f in range(faces):
                    at = f * cells + edge * last_row
                    grad[f, edge * (side - 1)] = acc[at:at + side].astype(BF16)


def shards(features, weight, out_bias, cotangent, seam_face, seam_edge, seam_flip):
    faces, side, _, width = features.shape
    nx, ny = lax.axis_size("fx"), lax.axis_size("fy")
    patch = (faces, side, side, width)
    padded = (faces, side + 2, side, width)
    strip = faces * side
    dma = pltpu.SemaphoreType.DMA
    hbm = pl.BlockSpec(memory_space=pltpu.HBM)
    vmem = pl.BlockSpec(memory_space=pltpu.VMEM)
    return pl.pallas_call(
        functools.partial(kernel, nx, ny, faces, side, width),
        out_shape=(jax.ShapeDtypeStruct(patch, BF16), jax.ShapeDtypeStruct(patch, BF16)),
        in_specs=[hbm] * 7,
        out_specs=(vmem, vmem),
        scratch_shapes=[
            pltpu.SMEM((4, faces), jnp.int32),
            pltpu.SMEM((4, faces), jnp.int32),
            pltpu.SMEM((4, faces), jnp.int32),
            pltpu.VMEM((1, width), F32),
            pltpu.VMEM(padded, BF16),
            pltpu.VMEM(patch, BF16),
            pltpu.VMEM((3, 3, width, width), BF16),
            pltpu.VMEM((faces * side * side, width), F32),
            pltpu.VMEM(padded, BF16),
            pltpu.VMEM((3 * width, 3 * width), BF16),
            pltpu.VMEM((2, width, 3 * width), BF16),
            pltpu.VMEM((3 * width, 3 * width), BF16),
            pltpu.VMEM((2, width, 3 * width), BF16),
            pltpu.VMEM((2, strip, width), F32),
            pltpu.VMEM((4, strip, width), F32),
            pltpu.VMEM((2, strip, strip), BF16),
            pltpu.VMEM((2, 2, 16, 256), BF16),
            pltpu.VMEM((2, 32, width), F32),
            pltpu.VMEM((2, 4, faces, side, width), BF16),
            pltpu.VMEM((2, 4, 16, width), BF16),
            pltpu.VMEM((2, 4, faces, side, width), BF16),
            pltpu.VMEM((2, 4, 16, width), BF16),
            pltpu.VMEM((8, faces + 2, side, width), BF16),
            pltpu.VMEM((8, faces + 2, side, width), BF16),
            dma((2, 8)),
            dma((2, 8)),
            dma((2, 2, 8)),
            dma((2, 3)),
            dma((2, 2, 8)),
            dma((2,)),
            dma((2, 2, 2)),
            dma((2, 2, 2)),
            dma((7,)),
        ],
        compiler_params=pltpu.CompilerParams(
            collective_id=0, has_side_effects=True, vmem_limit_bytes=40 * 1024 * 1024),
    )(*[pltpu.with_memory_space_constraint(value, pltpu.HBM) for value in (
        seam_face.T, seam_edge.T, seam_flip.T, out_bias.reshape(1, width), features, weight, cotangent)])


def solution(mesh):
    in_specs = (P(None, "fx", "fy", None), P(), P(), P(None, "fx", "fy", None), P(), P(), P())
    out_specs = (P(None, "fx", "fy", None), P(None, "fx", "fy", None))
    return jax.shard_map(shards, mesh=mesh, in_specs=in_specs, out_specs=out_specs, check_vma=False)
```

```python
import functools

import jax
import jax.numpy as jnp
from jax import lax
from jax.experimental import pallas as pl
from jax.experimental.pallas import tpu as pltpu
from jax.sharding import PartitionSpec as P

MESH = pl.DeviceIdType.MESH
F32 = jnp.float32
BF16 = jnp.bfloat16


def dot(a, b):
    return jnp.dot(a, b, preferred_element_type=F32)


def rows_iota(shape):
    return lax.broadcasted_iota(jnp.int32, shape, 0)


def cols_iota(shape):
    return lax.broadcasted_iota(jnp.int32, shape, 1)


def shifted_sum(taps, run):
    total, width = taps.shape[0], taps.shape[1] // 3
    place = rows_iota((total, width)) % run
    below = jnp.where(place == 0, 0.0, pltpu.roll(taps[:, :width], 1, 0))
    above = jnp.where(place == run - 1, 0.0, pltpu.roll(taps[:, 2 * width:], total - 1, 0))
    return taps[:, width:2 * width] + below + above


def silu_parts(value):
    sigma = 1.0 / (1.0 + jnp.exp(-value))
    return value * sigma, sigma * (1.0 + value * (1.0 - sigma))


def kernel(nx, ny, faces, side, width,
           face_hbm, edge_hbm, flip_hbm, bias_hbm, x_hbm, w_hbm, cot_hbm,
           act, grad,
           face_tab, edge_tab, flip_tab, bias_ref, xp, cot, w9, acc, sp,
           wf, wcol, vf, vcol, colcot, ring, turner, chooser, end_cells,
           src, corner_src, strip_in, corner_in, seam_first, seam_second,
           near_send, near_recv, seam_send, seam_recv, tail_send, relay_send, ends_send, ends_recv, load_sem):
    x = lax.axis_index("fx")
    y = lax.axis_index("fy")
    top, bottom, left, right = x == 0, x == nx - 1, y == 0, y == ny - 1
    on_rim = (top, bottom, left, right)
    row_rim = jnp.logical_or(top, bottom)
    col_rim = jnp.logical_or(left, right)
    rim = jnp.logical_or(row_rim, col_rim)
    corner = jnp.logical_and(row_rim, col_rim)
    seam = (seam_first, seam_second)
    cells = side * side
    strip = faces * side
    last_row = cells - side
    row_edge = x // (nx - 1)
    col_edge = 2 + y // (ny - 1)
    rims = ((row_rim, row_edge, y, ny, (y // (ny // 2)) * 4 + row_edge),
            (col_rim, col_edge, x, nx, (x // (nx // 2)) * 4 + col_edge))

    near = []
    for dx, dy, slot in ((-1, 0, 0), (1, 0, 1), (0, -1, 2), (0, 1, 3), (-1, -1, 4), (-1, 1, 5), (1, -1, 6), (1, 1, 7)):
        tx, ty = x + dx, y + dy
        inside = None
        for ok in ([tx >= 0] if dx < 0 else [tx < nx] if dx > 0 else []) + ([ty >= 0] if dy < 0 else [ty < ny] if dy > 0 else []):
            inside = ok if inside is None else jnp.logical_and(inside, ok)
        back = slot ^ 1 if slot < 4 else 4 + (3 - (slot - 4))
        near.append((tx, ty, inside, slot, back))

    def partners(which, tail=True):
        active, edge, place, count, slot = rims[which]
        for kind in range(2):
            for half in range(2):
                for turn in range(2):
                    spot = count - 1 - place if turn else place
                    tx, ty = (half * (nx - 1), spot) if kind == 0 else (spot, half * (ny - 1))
                    other = jnp.logical_not(jnp.logical_and(tx == x, ty == y))
                    on = jnp.logical_and(active, other)
                    if kind == 1:
                        on = jnp.logical_and(on, jnp.logical_not(corner))
                    by_relay = which == 0 and kind == 0 and turn == 1
                    if by_relay and not tail:
                        on = jnp.logical_and(on, jnp.logical_or(corner, half == row_edge))
                    yield kind * 4 + half * 2 + turn, tx, ty, on

    def near_copy(trip, item):
        tx, ty, inside, slot, back = item
        if slot < 4:
            source, target = src.at[trip, slot], strip_in.at[trip, back]
        else:
            source, target = corner_src.at[trip, slot - 4], corner_in.at[trip, back - 4]
        return pltpu.make_async_remote_copy(
            src_ref=source, dst_ref=target, send_sem=near_send.at[trip, slot], recv_sem=near_recv.at[trip, back],
            device_id=(tx, ty), device_id_type=MESH)

    def near_arrival(trip, slot):
        here = strip_in.at[trip, slot] if slot < 4 else corner_in.at[trip, slot - 4]
        return pltpu.make_async_copy(here, here, near_recv.at[trip, slot])

    def end_spot(which, edge, end):
        return 2 * edge + end if which == 0 else edge - 2 + 2 * end

    def has_next(which, end):
        place, count = rims[which][2], rims[which][3]
        return place < count - 1 if end else place > 0

    def seam_copy(trip, which, step, tx, ty, tail):
        slot = rims[which][4]
        line = seam[trip].at[slot, faces:faces + 2] if tail else seam[trip].at[slot, 0:faces]
        sems = tail_send if tail else seam_send
        straight = which == 0 and not tail and step < 4 and step % 2 == 0
        arrived = seam_recv.at[trip, 1 if tail else 0]
        if straight:
            arrived = seam_recv.at[trip, 2 * jnp.logical_not(corner).astype(jnp.int32)]
        return pltpu.make_async_remote_copy(
            src_ref=line, dst_ref=line, send_sem=sems.at[trip, which, step],
            recv_sem=arrived, device_id=(tx, ty), device_id_type=MESH)

    relays = jnp.logical_and(row_rim, jnp.logical_not(corner))

    def relay_line(trip):
        return seam[trip].at[(y // (ny // 2)) * 4 + 1 - row_edge, 0:faces]

    def relay_copy(trip):
        line = relay_line(trip)
        return pltpu.make_async_remote_copy(
            src_ref=line, dst_ref=line, send_sem=relay_send.at[trip],
            recv_sem=seam_recv.at[trip, 0], device_id=(x, ny - 1 - y), device_id_type=MESH)

    def send_relay(trip):
        @pl.when(relays)
        def _():
            line = relay_line(trip)
            pltpu.make_async_copy(line, line, seam_recv.at[trip, 2]).wait()
            relay_copy(trip).start()

    def end_copy(trip, which, end):
        active, edge, place, count, slot = rims[which]
        spot = place + 2 * end - 1
        tx, ty = (x, spot) if which == 0 else (spot, y)
        return pltpu.make_async_remote_copy(
            src_ref=corner_src.at[trip, end_spot(which, edge, end)],
            dst_ref=seam[trip].at[(spot // (count // 2)) * 4 + edge, faces + 1 - end],
            send_sem=ends_send.at[trip, which, end], recv_sem=ends_recv.at[trip, which, 1 - end],
            device_id=(tx, ty), device_id_type=MESH)

    def send_ends(trip, which):
        for end in range(2):
            @pl.when(jnp.logical_and(rims[which][0], has_next(which, end)))
            def _(end=end):
                end_copy(trip, which, end).start()

    def send_line(trip, which):
        for step, tx, ty, on in partners(which, False):
            @pl.when(on)
            def _(step=step, tx=tx, ty=ty):
                seam_copy(trip, which, step, tx, ty, False).start()

    def send_tails(trip):
        for which in range(2):
            active, edge, place, count, slot = rims[which]
            for end in range(2):
                @pl.when(jnp.logical_and(active, has_next(which, end)))
                def _(which=which, end=end, slot=slot):
                    here = seam[trip].at[slot, faces + end]
                    pltpu.make_async_copy(here, here, ends_recv.at[trip, which, end]).wait()
            for step, tx, ty, on in partners(which):
                @pl.when(on)
                def _(which=which, step=step, tx=tx, ty=ty):
                    seam_copy(trip, which, step, tx, ty, True).start()

    def send_near(trip, slots):
        for item in near:
            if item[3] in slots:
                @pl.when(item[2])
                def _(item=item):
                    near_copy(trip, item).start()

    def wait_sent(trip):
        @pl.when(rim)
        def _():
            for which in range(2):
                active = rims[which][0]
                for step, tx, ty, on in partners(which, False):
                    @pl.when(on)
                    def _(which=which, step=step, tx=tx, ty=ty):
                        seam_copy(trip, which, step, tx, ty, False).wait_send()
                for step, tx, ty, on in partners(which):
                    @pl.when(on)
                    def _(which=which, step=step, tx=tx, ty=ty):
                        seam_copy(trip, which, step, tx, ty, True).wait_send()
                for end in range(2):
                    @pl.when(jnp.logical_and(active, has_next(which, end)))
                    def _(which=which, end=end):
                        end_copy(trip, which, end).wait_send()
        @pl.when(relays)
        def _():
            relay_copy(trip).wait_send()
        for item in near:
            @pl.when(item[2])
            def _(item=item):
                near_copy(trip, item).wait_send()

    first_last = jnp.where(
        jnp.logical_and(
            cols_iota((32, strip)) == (rows_iota((32, strip)) % 16) * side + (rows_iota((32, strip)) // 16) * (side - 1),
            rows_iota((32, strip)) % 16 < faces),
        1.0, 0.0).astype(BF16)

    def prepare_choice():
        for which in range(2):
            active, edge, place, count, slot = rims[which]

            @pl.when(active)
            def _(which=which, edge=edge, place=place, count=count):
                row, col = rows_iota((strip, strip)), cols_iota((strip, strip))
                mirrored = row - 2 * (row % side) + (side - 1)
                end_row, end_col = rows_iota((16, 256)), cols_iota((16, 256))
                wanted = row
                chosen = [jnp.zeros((16, 256), F32)] * 2
                for f in range(faces):
                    flip = flip_tab[edge, f]
                    flipped = jnp.logical_and(row // side == f, jnp.full((strip, strip), flip, jnp.int32) == 1)
                    wanted = jnp.where(flipped, mirrored, wanted)
                    part = place // (count // 2)
                    part = part + flip * (1 - 2 * part)
                    for end in range(2):
                        code = ((part * 4 + edge_tab[edge, f]) * 2 + end + flip * (1 - 2 * end)) * 16 + face_tab[edge, f]
                        hit = jnp.logical_and(end_row == f, end_col == code)
                        chosen[end] = jnp.where(hit, 1.0, chosen[end])
                turner[which] = jnp.where(wanted == col, 1.0, 0.0).astype(BF16)
                for end in range(2):
                    chooser[which, end] = chosen[end].astype(BF16)

    def seam_arrivals(trip):
        def wait_for(lines, tails):
            here = seam[trip].at[0:lines, 0:faces]
            pltpu.make_async_copy(here, here, seam_recv.at[trip, 0]).wait()
            here = seam[trip].at[0:tails, 0:2]
            pltpu.make_async_copy(here, here, seam_recv.at[trip, 1]).wait()

        @pl.when(corner)
        def _():
            wait_for(6, 6)

        @pl.when(relays)
        def _():
            wait_for(6, 7)

        @pl.when(jnp.logical_not(row_rim))
        def _():
            wait_for(7, 7)
        for which in range(2):
            active, edge, place, count, slot = rims[which]

            @pl.when(active)
            def _(which=which, edge=edge, place=place, count=count):
                part = place // (count // 2)
                lines = []
                for f in range(faces):
                    flip = flip_tab[edge, f]
                    lines.append(seam[trip][(part + flip * (1 - 2 * part)) * 4 + edge_tab[edge, f], face_tab[edge, f]])
                line = dot(turner[which], jnp.concatenate(lines, axis=0)).astype(BF16)
                strip_in[trip, edge] = line.reshape(faces, side, width)
                if trip == 0:
                    @pl.when(corner)
                    def _():
                        end_cells[which] = dot(first_last, line)
                offered = jnp.concatenate(
                    [seam[trip][slot, faces + end] for slot in range(8) for end in range(2)], axis=0)
                for end in range(2):
                    value = dot(chooser[which, end], offered).astype(BF16)

                    @pl.when(has_next(which, end))
                    def _(end=end, value=value):
                        corner_in[trip, end_spot(which, edge, end)] = value

    load_x = pltpu.make_async_copy(x_hbm, xp.at[:, 1:side + 1], load_sem.at[0])
    load_w = pltpu.make_async_copy(w_hbm, w9, load_sem.at[1])
    load_c = pltpu.make_async_copy(cot_hbm, cot, load_sem.at[2])
    loads = [pltpu.make_async_copy(there, here, load_sem.at[3 + i]) for i, (there, here) in enumerate(
        ((face_hbm, face_tab), (edge_hbm, edge_tab), (flip_hbm, flip_tab), (bias_hbm, bias_ref)))]
    load_rows = [pltpu.make_async_copy(x_hbm.at[:, half * (side - 1)], src.at[0, half], load_sem.at[7 + half])
                 for half in range(2)]
    for load in load_rows:
        load.start()
    load_x.start()
    load_w.start()
    for load in loads:
        load.start()
    load_c.start()

    barrier = pltpu.get_barrier_semaphore()
    due = jnp.int32(0)

    def greet(on, tx, ty):
        @pl.when(on)
        def _():
            pl.semaphore_signal(barrier, inc=1, device_id=(tx, ty), device_id_type=MESH)
        return on.astype(jnp.int32)

    for which in range(2):
        for step, tx, ty, on in partners(which):
            due = due + greet(jnp.logical_and(on, jnp.logical_not(corner)) if which else on, tx, ty)
    for tx, ty, inside, slot, back in near:
        due = due + greet(inside, tx, ty)

    zero_rows = jnp.zeros((faces, side, width), BF16)
    zero_tile = jnp.zeros((side, width), BF16)
    for which in range(2):
        for end in range(2):
            @pl.when(jnp.logical_and(rims[which][0], jnp.logical_not(has_next(which, end))))
            def _(which=which, end=end):
                for trip in range(2):
                    seam[trip][rims[which][4], faces + end] = zero_tile
    for half in range(2):
        load_rows[half].wait()
        line = src[0, half]
        picked = dot(first_last, line.reshape(strip, width)).astype(BF16)
        corner_src[0, 2 * half] = picked[:16]
        corner_src[0, 2 * half + 1] = picked[16:]

        @pl.when(on_rim[half])
        def _(line=line):
            seam[0][rims[0][4], 0:faces] = line
    pl.semaphore_wait(barrier, due)
    send_ends(0, 0)
    send_ends(0, 1)
    send_line(0, 0)
    send_near(0, (0, 1, 4, 5, 6, 7))
    load_x.wait()
    column_pick = jnp.where(
        cols_iota((2 * side, cells)) == (rows_iota((2 * side, cells)) % side) * side
        + (rows_iota((2 * side, cells)) // side) * (side - 1), 1.0, 0.0).astype(BF16)
    for f in range(faces):
        both = dot(column_pick, xp[f, 1:side + 1].reshape(cells, width)).astype(BF16)
        src[0, 2, f] = both[:side]
        src[0, 3, f] = both[side:]

    @pl.when(col_rim)
    def _():
        seam[0][rims[1][4], 0:faces] = src[0, col_edge]
    send_line(0, 1)
    send_near(0, (2, 3))
    send_tails(0)

    xp[:, 0] = zero_rows
    xp[:, side + 1] = zero_rows
    sp[:, 0] = zero_rows
    sp[:, side + 1] = zero_rows

    load_w.wait()
    for a in range(3):
        for b in range(3):
            tap = w9[a, b]
            back = tap.astype(F32).T.astype(BF16)
            wf[a * width:(a + 1) * width, b * width:(b + 1) * width] = tap
            vf[(2 - a) * width:(3 - a) * width, (2 - b) * width:(3 - b) * width] = back
            if b != 1:
                wcol[b // 2, :, a * width:(a + 1) * width] = tap
                vcol[b // 2, :, (2 - a) * width:(3 - a) * width] = back
    for load in loads:
        load.wait()
    prepare_choice()
    load_c.wait()
    for f in range(faces):
        both = dot(column_pick, cot[f].reshape(cells, width))
        colcot[0, f * side:(f + 1) * side] = both[:side]
        colcot[1, f * side:(f + 1) * side] = both[side:]

    def conv(source, f, weights):
        stacked = jnp.concatenate(
            [source[f, a:a + side].reshape(cells, width) for a in range(3)], axis=1)
        return shifted_sum(dot(stacked, weights), side)

    def forward_face(f, carry):
        acc[pl.ds(pl.multiple_of(f * cells, cells), cells)] = conv(xp, f, wf[...]) + bias_ref[...]
        return carry
    send_relay(0)
    lax.fori_loop(0, faces, forward_face, 0)

    def add_strip(edge, value):
        if edge < 2:
            for f in range(faces):
                at = f * cells + edge * last_row
                acc[at:at + side] += value[f * side:(f + 1) * side]
        else:
            at = pl.ds((edge - 2) * (side - 1), strip, stride=side)
            acc[at] = acc[at] + value

    def corner_at(v, h):
        return pl.ds(v * last_row + h * (side - 1), faces, stride=cells)

    def add_corner(v, h, value):
        acc[corner_at(v, h)] = acc[corner_at(v, h)] + value

    def forward_strip(edge):
        line = strip_in[0, edge].reshape(strip, width)
        weights = wf[2 * edge * width:(2 * edge + 1) * width] if edge < 2 else wcol[edge - 2]
        add_strip(edge, shifted_sum(dot(line, weights), side))

    def forward_corner(v, h):
        add_corner(v, h, dot(corner_in[0, 2 * v + h], w9[2 * v, 2 * h])[:faces])

    def from_near(trip, strip_step, corner_step):
        for item in near:
            @pl.when(item[2])
            def _(item=item):
                near_arrival(trip, item[3]).wait()
                if item[3] < 4:
                    strip_step(item[3])
                else:
                    corner_step((item[3] - 4) // 2, item[3] % 2)

    corner_pairs = [(v, h) for v in range(2) for h in range(2)]

    def at_both(v, h):
        return jnp.logical_and(bottom if v else top, right if h else left)

    from_near(0, forward_strip, forward_corner)

    @pl.when(rim)
    def _():
        seam_arrivals(0)
        for v, h in corner_pairs:
            @pl.when(at_both(v, h))
            def _(v=v, h=h):
                total = end_cells[0, 16 * h:16 * h + 16] + end_cells[1, 16 * v:16 * v + 16]
                corner_in[0, 2 * v + h] = (0.5 * total).astype(BF16)
        for edge in range(4):
            @pl.when(on_rim[edge])
            def _(edge=edge):
                forward_strip(edge)
        for v, h in corner_pairs:
            @pl.when(jnp.logical_or(bottom if v else top, right if h else left))
            def _(v=v, h=h):
                forward_corner(v, h)

    def ring_strip(edge):
        if edge < 2:
            at = edge * last_row
            line = jnp.concatenate([acc[f * cells + at:f * cells + at + side] for f in range(faces)], axis=0)
            turned_cot = cot[:, edge * (side - 1)].reshape(strip, width).astype(F32)
            weights = vf[2 * (1 - edge) * width:(2 * (1 - edge) + 1) * width]
        else:
            line = acc[pl.ds((edge - 2) * (side - 1), strip, stride=side)]
            turned_cot = colcot[edge - 2]
            weights = vcol[edge - 2]
        slope = (turned_cot * silu_parts(line)[1]).astype(BF16)
        return shifted_sum(dot(slope, weights), side)

    beyond = []
    for v, h in corner_pairs:
        slope = colcot.at[h][pl.ds(v * (side - 1), faces, stride=side)] * silu_parts(acc[corner_at(v, h)])[1]
        slope = jnp.concatenate([slope, jnp.zeros((16 - faces, width), F32)], axis=0).astype(BF16)
        value = dot(slope, vf[2 * (1 - v) * width:(2 * (1 - v) + 1) * width, 2 * (1 - h) * width:(2 * (1 - h) + 1) * width])
        beyond.append(value)
        corner_src[1, 2 * v + h] = value.astype(BF16)

    send_ends(1, 0)
    send_ends(1, 1)

    @pl.when(rim)
    def _():
        for edge in range(4):
            @pl.when(on_rim[edge])
            def _(edge=edge):
                ring[edge] = ring_strip(edge)
        for v, h in corner_pairs:
            @pl.when(at_both(v, h))
            def _(v=v, h=h):
                along_row = pl.ds(h * (side - 1), faces, stride=side)
                along_col = pl.ds(v * (side - 1), faces, stride=side)
                ring[v, along_row] = ring[v, along_row] + 0.5 * beyond[2 * v + h][:faces]
                ring[2 + h, along_col] = ring[2 + h, along_col] + 0.5 * beyond[2 * v + h][:faces]
        for which in range(2):
            active, edge, place, count, slot = rims[which]

            @pl.when(active)
            def _(edge=edge, slot=slot):
                seam[1][slot, 0:faces] = ring[edge].astype(BF16).reshape(faces, side, width)
            send_line(1, which)
    for edge in range(4):
        @pl.when(jnp.logical_not(on_rim[edge]))
        def _(edge=edge):
            src[1, edge] = ring_strip(edge).astype(BF16).reshape(faces, side, width)
    send_tails(1)
    send_near(1, range(8))

    def adjoint_face(f, carry):
        at = pl.ds(pl.multiple_of(f * cells, cells), cells)
        value, slope = silu_parts(acc[at])
        act[f] = value.astype(BF16).reshape(side, side, width)
        slope = cot[f].reshape(cells, width).astype(F32) * slope
        sp[f, 1:side + 1] = slope.astype(BF16).reshape(side, side, width)
        acc[at] = conv(sp, f, vf[...])
        return carry
    lax.fori_loop(0, faces // 3, adjoint_face, 0)
    send_relay(1)
    lax.fori_loop(faces // 3, faces, adjoint_face, 0)

    def adjoint_strip(edge):
        add_strip(edge, strip_in[1, edge].reshape(strip, width).astype(F32))

    def adjoint_corner(v, h):
        add_corner(v, h, corner_in[1, 2 * v + h].astype(F32)[:faces])

    def finish_face(f, carry):
        at = pl.ds(pl.multiple_of(f * cells, cells), cells)
        grad[f] = acc[at].astype(BF16).reshape(side, side, width)
        return carry

    wait_sent(0)
    from_near(1, adjoint_strip, adjoint_corner)

    @pl.when(jnp.logical_not(col_rim))
    def _():
        lax.fori_loop(0, faces, finish_face, 0)
    wait_sent(1)

    @pl.when(rim)
    def _():
        seam_arrivals(1)
        for edge in range(4):
            @pl.when(on_rim[edge])
            def _(edge=edge):
                adjoint_strip(edge)
        for v, h in corner_pairs:
            vertical, horizontal = bottom if v else top, right if h else left

            @pl.when(vertical != horizontal)
            def _(v=v, h=h):
                adjoint_corner(v, h)

        @pl.when(col_rim)
        def _():
            lax.fori_loop(0, faces, finish_face, 0)
        for edge in range(2):
            @pl.when(jnp.logical_and(on_rim[edge], jnp.logical_not(col_rim)))
            def _(edge=edge):
                for f in range(faces):
                    at = f * cells + edge * last_row
                    grad[f, edge * (side - 1)] = acc[at:at + side].astype(BF16)


def shards(features, weight, out_bias, cotangent, seam_face, seam_edge, seam_flip):
    faces, side, _, width = features.shape
    nx, ny = lax.axis_size("fx"), lax.axis_size("fy")
    patch = (faces, side, side, width)
    padded = (faces, side + 2, side, width)
    strip = faces * side
    dma = pltpu.SemaphoreType.DMA
    hbm = pl.BlockSpec(memory_space=pltpu.HBM)
    vmem = pl.BlockSpec(memory_space=pltpu.VMEM)
    return pl.pallas_call(
        functools.partial(kernel, nx, ny, faces, side, width),
        out_shape=(jax.ShapeDtypeStruct(patch, BF16), jax.ShapeDtypeStruct(patch, BF16)),
        in_specs=[hbm] * 7,
        out_specs=(vmem, vmem),
        scratch_shapes=[
            pltpu.SMEM((4, faces), jnp.int32),
            pltpu.SMEM((4, faces), jnp.int32),
            pltpu.SMEM((4, faces), jnp.int32),
            pltpu.VMEM((1, width), F32),
            pltpu.VMEM(padded, BF16),
            pltpu.VMEM(patch, BF16),
            pltpu.VMEM((3, 3, width, width), BF16),
            pltpu.VMEM((faces * side * side, width), F32),
            pltpu.VMEM(padded, BF16),
            pltpu.VMEM((3 * width, 3 * width), BF16),
            pltpu.VMEM((2, width, 3 * width), BF16),
            pltpu.VMEM((3 * width, 3 * width), BF16),
            pltpu.VMEM((2, width, 3 * width), BF16),
            pltpu.VMEM((2, strip, width), F32),
            pltpu.VMEM((4, strip, width), F32),
            pltpu.VMEM((2, strip, strip), BF16),
            pltpu.VMEM((2, 2, 16, 256), BF16),
            pltpu.VMEM((2, 32, width), F32),
            pltpu.VMEM((2, 4, faces, side, width), BF16),
            pltpu.VMEM((2, 4, 16, width), BF16),
            pltpu.VMEM((2, 4, faces, side, width), BF16),
            pltpu.VMEM((2, 4, 16, width), BF16),
            pltpu.VMEM((8, faces + 2, side, width), BF16),
            pltpu.VMEM((8, faces + 2, side, width), BF16),
            dma((2, 8)),
            dma((2, 8)),
            dma((2, 2, 8)),
            dma((2, 3)),
            dma((2, 2, 8)),
            dma((2,)),
            dma((2, 2, 2)),
            dma((2, 2, 2)),
            dma((9,)),
        ],
        compiler_params=pltpu.CompilerParams(
            collective_id=0, has_side_effects=True, vmem_limit_bytes=40 * 1024 * 1024),
    )(*[pltpu.with_memory_space_constraint(value, pltpu.HBM) for value in (
        seam_face.T, seam_edge.T, seam_flip.T, out_bias.reshape(1, width), features, weight, cotangent)])


def solution(mesh):
    in_specs = (P(None, "fx", "fy", None), P(), P(), P(None, "fx", "fy", None), P(), P(), P())
    out_specs = (P(None, "fx", "fy", None), P(None, "fx", "fy", None))
    return jax.shard_map(shards, mesh=mesh, in_specs=in_specs, out_specs=out_specs, check_vma=False)
```
